256 devices in a mesh: seq: 32 (over y, x, core), head: 8 (over z).
Axes of the slice: x: 4, y: 4, z: 8, core: 2. Of those that a mesh axis runs over, the one named last changes fastest.
Arguments:
- queries: bfloat16 [16384, 4096], P('seq', 'head'), may hold values from -6 to 6
- keys: bfloat16 [16384, 4096], P('seq', 'head'), may hold values from -6 to 6
- values: bfloat16 [16384, 4096], P('seq', 'head'), may hold values from -6 to 6
- log_decay: float32 [32, 16384], P('head', 'seq'), may hold values from -1 to 0
- out_weight: bfloat16 [4096, 3072], P('head'), may hold values from -0.09375 to 0.09375
- grad_out: bfloat16 [16384, 3072], P('seq', 'head'), may hold values from -0.0625 to 0.0625
Outputs:
- grad_q: float32 [16384, 4096], P('seq', 'head')
- grad_k: float32 [16384, 4096], P('seq', 'head')
- grad_v: float32 [16384, 4096], P('seq', 'head')
The draws below stay inside these ranges and needn't reach their ends.
All inputs are finite; a program needn't handle non-finite values.
Results may differ from the reference program's by a relative error of at most 0.003.
Values may be sent and summed in bfloat16 or wider, within the bound.
No kernel may reach another device: no remote copies, remote signals or barrier semaphores. Data moves between devices by JAX's collectives and lax.ppermute only.
A program may use at most 128 MiB of HBM per device.

```python
import math
import jax
import jax.numpy as jnp
from jax import lax

D = 3072
DH = 128
TOK_DEV = 512
HEADS = 32
QKV = 4096
TOKENS = 16384


def draw_log_decay(key, part):
    key = jax.random.fold_in(key, 7)
    key_slow, key_fast, key_rank, coarse_random_seed, key_spot, key_amount = jax.random.split(key, 6)
    gentle_decline = jax.random.uniform(key_slow, (HEADS, 1), minval=0.1, maxval=0.6) / TOKENS
    fast_rate = jnp.exp(jax.random.uniform(key_fast, (HEADS, 1), minval=math.log(1.0 / 50.0), maxval=math.log(1.0 / 30.0)))
    ranks = jax.random.permutation(key_rank, HEADS)
    fast_count = HEADS // 2
    is_fast = (ranks < fast_count)[:, None]
    rough = jax.random.uniform(coarse_random_seed, (HEADS, TOKENS), minval=0.5, maxval=1.5)
    starting_shift = -jnp.where(is_fast, fast_rate, gentle_decline) * rough
    marked_locations = jax.random.randint(key_spot, (HEADS, 3), 0, TOKENS)
    magnitude_entries = jax.random.uniform(key_amount, (HEADS, 3), minval=0.15, maxval=0.3)
    location_numbers = jnp.arange(TOKENS)
    cluster_sets = jnp.sum(jnp.where(location_numbers[None, None, :] == marked_locations[:, :, None], magnitude_entries[:, :, None], 0.0), axis=1)
    return (starting_shift - cluster_sets).astype(jnp.float32)


def levels(key, shape, cuts, smallest, largest):
    def one(dim, blocks):
        draws = jax.random.uniform(jax.random.fold_in(jax.random.fold_in(key, 6), dim), (blocks,), jnp.float32, smallest / len(cuts), largest / len(cuts))
        return jnp.repeat(jnp.exp(draws), shape[dim] // blocks).reshape((-1,) + (1,) * (len(shape) - dim - 1))

    gain = one(*cuts[0])
    for cut in cuts[1:]:
        gain = gain * one(*cut)
    return gain


def bell_draw(rng, dims, spread, reach, cuts=(), kind=jnp.bfloat16):
    level = levels(rng, dims, cuts, -0.22, 0.18) if cuts else 1.0
    entries = jax.random.normal(rng, dims, jnp.float32) * spread * level
    return jnp.minimum(jnp.maximum(entries, -reach), reach).astype(kind)


def setup_inputs(seed: int = 0) -> dict:
    key_list = jax.random.split(jax.random.key(seed), 7)
    queries = bell_draw(key_list[0], (TOKENS, QKV), 1.0, 6.0, ((0, 32), (1, 8)))
    keys = bell_draw(key_list[1], (TOKENS, QKV), 1.0, 6.0, ((0, 32), (1, 8)))
    values = bell_draw(key_list[2], (TOKENS, QKV), 1.0, 6.0, ((0, 32), (1, 8)))
    log_decay = draw_log_decay(jax.random.fold_in(key_list[6], 71), 0)
    out_weight = bell_draw(key_list[4], (QKV, D), QKV ** -0.5, 0.09375, ((0, 8),))
    grad_out = bell_draw(key_list[5], (TOKENS, D), (0.5 / TOKENS ** 0.5), 0.0625, ((0, 32), (1, 8)))
    return dict(queries=queries, keys=keys, values=values, log_decay=log_decay, out_weight=out_weight, grad_out=grad_out)


def local_terms(queries, keys, values, grad_attn, log_decay):
    head_size = queries.shape[-1]
    running = jnp.cumsum(log_decay, axis=1)
    location_numbers = jnp.arange(running.shape[1])
    causal = location_numbers[:, None] >= location_numbers[None, :]
    decay_mask = jnp.exp(jnp.where(causal[None], running[:, :, None] - running[:, None, :], -jnp.inf)) / head_size
    query_wide = queries.astype(jnp.float32)
    k_wide = keys.astype(jnp.float32)
    v_wide = values.astype(jnp.float32)
    g_wide = grad_attn.astype(jnp.float32)
    scores = (jnp.einsum("thd,shd->hts", query_wide, k_wide) * decay_mask).astype(jnp.bfloat16).astype(jnp.float32)
    grad_scores = (jnp.einsum("the,she->hts", g_wide, v_wide) * decay_mask).astype(jnp.bfloat16).astype(jnp.float32)
    query_gradient_local = jnp.einsum("hts,shd->thd", grad_scores, k_wide)
    dk_local = jnp.einsum("hts,thd->shd", grad_scores, query_wide)
    dv_local = jnp.einsum("hts,the->she", scores, g_wide)
    to_end = jnp.exp(running[:, -1:] - running)
    from_start = jnp.exp(running)
    key_state = jnp.einsum("thd,the->hde", k_wide * to_end.T[:, :, None], v_wide, precision=lax.Precision.HIGHEST)
    grad_state = jnp.einsum("thd,the->hde", query_wide * from_start.T[:, :, None], g_wide, precision=lax.Precision.HIGHEST)
    return (query_gradient_local, dk_local, dv_local, to_end, from_start), key_state, grad_state, running[:, -1]


def finish(queries, keys, values, grad_attn, parts, state_in, state_out):
    query_gradient_local, dk_local, dv_local, to_end, from_start = parts
    head_size = state_in.shape[-1]
    start_w = (from_start.T / head_size)[:, :, None]
    end_w = (to_end.T / head_size)[:, :, None]
    high = lax.Precision.HIGHEST
    grad_q = query_gradient_local + start_w * jnp.einsum("the,hde->thd", grad_attn.astype(jnp.float32), state_in, precision=high)
    grad_k = dk_local + end_w * jnp.einsum("the,hde->thd", values.astype(jnp.float32), state_out, precision=high)
    grad_v = dv_local + end_w * jnp.einsum("thd,hde->the", keys.astype(jnp.float32), state_out, precision=high)
    return grad_q, grad_k, grad_v


def reference(queries, keys, values, log_decay, out_weight, grad_out):
    blocks = TOKENS // TOK_DEV
    grad_attn = lax.dot_general(grad_out, out_weight, (((1,), (1,)), ((), ())), preferred_element_type=jnp.float32).astype(jnp.bfloat16)

    def split(array):
        return array.reshape(blocks, TOK_DEV, HEADS, DH)

    decay_blocks = log_decay.reshape(HEADS, blocks, TOK_DEV).transpose(1, 0, 2)
    inputs = (split(queries), split(keys), split(values), split(grad_attn))

    def open_block(item):
        return local_terms(*item)

    parts, seed_collection, grad_states, totals = lax.map(open_block, inputs + (decay_blocks,))

    def forward(carry, item):
        state, total = item
        return carry * jnp.exp(total)[:, None, None] + state, carry

    def backward(carry, item):
        state, total = item
        return state + jnp.exp(total)[:, None, None] * carry, carry

    zeros = jnp.zeros((HEADS, DH, DH), jnp.float32)
    final_key, states_in = lax.scan(forward, zeros, (seed_collection, totals))
    final_grad, states_out = lax.scan(backward, zeros, (grad_states, totals), reverse=True)

    def close_block(item):
        return finish(*item)

    grad_q, grad_k, grad_v = lax.map(close_block, inputs + (parts, states_in, states_out))
    return (grad_q.reshape(TOKENS, HEADS * DH), grad_k.reshape(TOKENS, HEADS * DH),
            grad_v.reshape(TOKENS, HEADS * DH))
```

```python
import functools

import jax
import jax.numpy as jnp
from jax import lax
from jax.experimental import pallas as pl
from jax.experimental.pallas import tpu as pltpu
from jax.sharding import PartitionSpec as P

DH = 128
NT = (((1,), (1,)), ((), ()))
NN = (((1,), (0,)), ((), ()))
TN = (((0,), (0,)), ((), ()))
VMEM = pl.BlockSpec(memory_space=pltpu.VMEM)
ANY = pl.BlockSpec(memory_space=pl.ANY)
SMEM = pl.BlockSpec(memory_space=pltpu.SMEM)


def dot(a, b, dims):
    return lax.dot_general(a, b, dims, preferred_element_type=jnp.float32)


def pieces(x, n):
    out = []
    for _ in range(n):
        p = x.astype(jnp.bfloat16)
        out.append(p)
        x = x - p.astype(jnp.float32)
    return out


def call(kernel, outs, *args, specs=None, limit=24, scratch=(), aliases=None):
    return pl.pallas_call(
        kernel,
        out_shape=outs,
        in_specs=specs or [VMEM] * len(args),
        out_specs=tuple(VMEM for _ in outs),
        scratch_shapes=scratch,
        input_output_aliases=aliases or {},
        compiler_params=pltpu.CompilerParams(vmem_limit_bytes=limit * 2**20),
    )(*args)


def f32(*shape):
    return jax.ShapeDtypeStruct(shape, jnp.float32)


def bf16(*shape):
    return jax.ShapeDtypeStruct(shape, jnp.bfloat16)


def running(ld):
    n = ld.shape[1]
    s = lax.broadcasted_iota(jnp.int32, (n, n), 0)
    t = lax.broadcasted_iota(jnp.int32, (n, n), 1)
    upto = jnp.where(s <= t, 1.0, 0.0).astype(jnp.bfloat16)
    parts = pieces(ld, 3)
    return sum(dot(p, upto, NN) for p in parts), sum(dot(p, jnp.ones((n, DH), jnp.bfloat16), NN) for p in parts)


def running_columns(ld):
    n = ld.shape[1]
    s = lax.broadcasted_iota(jnp.int32, (n, n), 0)
    t = lax.broadcasted_iota(jnp.int32, (n, n), 1)
    since = jnp.where(s >= t, 1.0, 0.0).astype(jnp.bfloat16)
    return sum(dot(since, p, NT) for p in pieces(ld, 3))


def open_kernel(heads, k_hbm, v_hbm, ld_ref, tie_ref, state_ref, tied_ref, k_ref, v_ref, sems):
    copies = [pltpu.make_async_copy(src, dst, sems.at[i]) for i, (src, dst) in enumerate(((k_hbm, k_ref), (v_hbm, v_ref)))]
    for copy in copies:
        copy.start()
    tied_ref[...] = tie_ref[...]
    n = k_ref.shape[0]
    row, total = running(ld_ref[...])
    state_ref[pl.ds(heads * DH, heads), :] = total
    state_ref[pl.ds(heads * DH + heads, 8 - heads), :] = jnp.zeros((8 - heads, DH), jnp.float32)
    for copy in copies:
        copy.wait()
    for h in range(heads):
        cols = slice(h * DH, (h + 1) * DH)
        kt = k_ref[:, cols].T.astype(jnp.float32) * jnp.exp(row[h : h + 1, n - 1 : n] - row[h : h + 1, :])
        hi, lo = pieces(kt, 2)
        v = v_ref[:, cols]
        state_ref[pl.ds(h * DH, DH), :] = dot(hi, v, NN) + dot(lo, v, NN)


def local_kernel(heads, first, q_ref, k_ref, v_ref, ga_ref, row_ref, col_ref, dq_ref, dk_ref, dv_ref, start_ref, end_ref, tie_ref):
    n = q_ref.shape[0]
    step = n // 2
    s = lax.broadcasted_iota(jnp.int32, (step, step), 0)
    t = lax.broadcasted_iota(jnp.int32, (step, step), 1)
    keep = s <= t
    for i in range(heads):
        h = first + i
        cols, to = slice(h * DH, (h + 1) * DH), slice(i * DH, (i + 1) * DH)
        col = col_ref[:, h : h + 1]
        start_ref[:, to] = jnp.broadcast_to(jnp.exp(col) * (1.0 / DH), (n, DH))
        end_ref[:, to] = jnp.broadcast_to(jnp.exp(row_ref[h : h + 1, n - 1 : n] - col) * (1.0 / DH), (n, DH))
        for sb in range(2):
            srows = slice(sb * step, (sb + 1) * step)
            k, v = k_ref[srows, cols], v_ref[srows, cols]
            col = col_ref[srows, h : h + 1]
            dk = dv = None
            for tb in range(sb, 2):
                trows = slice(tb * step, (tb + 1) * step)
                q, ga = q_ref[trows, cols], ga_ref[trows, cols]
                gap = row_ref[h : h + 1, trows] - col
                if tb == sb:
                    gap = jnp.where(keep, gap, -jnp.inf)
                weight = jnp.exp(gap) * (1.0 / DH)
                scores = (dot(k, q, NT) * weight).astype(jnp.bfloat16)
                grads = (dot(v, ga, NT) * weight).astype(jnp.bfloat16)
                dv_part = dot(scores, ga, NN)
                dk_part = dot(grads, q, NN)
                dv = dv_part if dv is None else dv + dv_part
                dk = dk_part if dk is None else dk + dk_part
                dq = dot(grads, k, TN)
                if sb == 0:
                    dq_ref[trows, to] = dq
                else:
                    dq_ref[trows, to] += dq
            dk_ref[srows, to] = dk
            dv_ref[srows, to] = dv
    tie_ref[...] = jnp.zeros(tie_ref.shape, jnp.float32)


def first_kernel(
    place_ref, w_hbm, c_hbm, q_hbm, ld_ref, a1, b1, a2, b2,
    acc_ref, w_ref, qw_ref, row_ref, col_ref, near_ref, c_ref, q_ref, sems,
):
    z, side = place_ref[0], 1 - 2 * place_ref[1]
    rows, width = c_ref.shape
    heads = ld_ref.shape[0]
    targets = [near_ref.at[i] for i in range(5)] + [w_ref.at[i] for i in range(3)]
    copies = [pltpu.make_async_copy(c_hbm, c_ref, sems.at[8]), pltpu.make_async_copy(q_hbm, q_ref, sems.at[9])]
    for i, (offset, target) in enumerate(zip((0, -1, 1, -2, 2, -3, 3, 4), targets)):
        at = lax.rem(z + offset * side + 8, 8) * width
        copies.append(pltpu.make_async_copy(w_hbm.at[:, pl.ds(pl.multiple_of(at, 128), width)], target, sems.at[i]))
    for copy in copies:
        copy.start()
    row, _ = running(ld_ref[...])
    row_ref[...] = row
    col_ref[...] = running_columns(ld_ref[...])
    copies[1].wait()
    for h in range(heads):
        qt = q_ref[:, h * DH : (h + 1) * DH].T.astype(jnp.float32) * jnp.exp(row[h : h + 1, :])
        hi, lo = pieces(qt, 2)
        qw_ref[h, :DH, :] = hi
        qw_ref[h, DH:, :] = lo
    copies[0].wait()
    for copy in copies[2:]:
        copy.wait()
    half = rows // 2
    for part in range(2):
        at = pl.ds(part * half, half)
        acc = dot(c_ref[at, :], near_ref[0], NT)
        for i, ref in enumerate((a1, b1, a2, b2)):
            acc += dot(ref[at, :], near_ref[i + 1], NT)
        acc_ref[at, :] = acc


def second_kernel(acc_ref, a3, b3, w_ref, out_ref):
    half = acc_ref.shape[0] // 2
    for part in range(2):
        at = pl.ds(part * half, half)
        out_ref[at, :] = acc_ref[at, :] + dot(a3[at, :], w_ref[0], NT) + dot(b3[at, :], w_ref[1], NT)


def late_kernel(heads, acc_ref, a4, w_ref, qw_ref, ga_ref, state_ref):
    half = acc_ref.shape[0] // 2
    for part in range(2):
        at = pl.ds(part * half, half)
        ga_ref[at, :] = (acc_ref[at, :] + dot(a4[at, :], w_ref[2], NT)).astype(jnp.bfloat16)
    for h in range(heads):
        both = dot(qw_ref[h], ga_ref[:, h * DH : (h + 1) * DH], NN)
        state_ref[pl.ds(h * DH, DH), :] = both[:DH] + both[DH:]


def one_row(tile, i):
    return jnp.sum(jnp.where(lax.broadcasted_iota(jnp.int32, tile.shape, 0) == i, tile, 0.0), axis=0, keepdims=True)


def tail_of(totals):
    parts = [[p.astype(jnp.float32) for p in pieces(t, 3)] for t in totals]
    at = lax.broadcasted_iota(jnp.int32, (16, DH), 0)
    out = jnp.zeros((16, DH), jnp.float32)
    for j, three in enumerate(parts):
        for i, part in enumerate(three):
            out = jnp.where(at == 3 * j + i, part, out)
    return out.astype(jnp.bfloat16)


def total_in(tail, j):
    tail = tail.astype(jnp.float32)
    return one_row(tail, 3 * j) + one_row(tail, 3 * j + 1) + one_row(tail, 3 * j + 2)


def chip_key_kernel(heads, place_ref, key_ref, key_other, tie_ref, sent_ref, chip_ref, tied_ref):
    tied_ref[...] = tie_ref[...]
    core = place_ref[1]
    pair = heads // 2
    first = core == 0
    totals = []
    for j in range(pair):
        h = core * pair + j
        mine = one_row(key_ref[heads * DH :, :], h)
        others = one_row(key_other[heads * DH :, :], h)
        totals.append(mine + others)
        at = pl.ds(pl.multiple_of(h * DH, DH), DH)
        key = jnp.where(first, jnp.exp(others), 1.0) * key_ref[at, :] + jnp.where(first, 1.0, jnp.exp(mine)) * key_other[at, :]
        chip_ref[pl.ds(j * DH, DH), :] = key
        sent_ref[pl.ds(j * DH, DH), :] = key.astype(jnp.bfloat16)
    sent_ref[pl.ds(pair * DH, 16), :] = tail_of(totals)


def chip_grad_kernel(heads, place_ref, key_ref, key_other, grad_ref, grad_other, sent_ref, chip_ref):
    core = place_ref[1]
    pair = heads // 2
    first = core == 0
    for j in range(pair):
        h = core * pair + j
        mine = jnp.exp(one_row(key_ref[heads * DH :, :], h))
        others = jnp.exp(one_row(key_other[heads * DH :, :], h))
        at = pl.ds(pl.multiple_of(h * DH, DH), DH)
        grad = jnp.where(first, 1.0, others) * grad_ref[at, :] + jnp.where(first, mine, 1.0) * grad_other[at, :]
        chip_ref[pl.ds(j * DH, DH), :] = grad
        sent_ref[pl.ds(j * DH, DH), :] = grad.astype(jnp.bfloat16)


def flag(condition):
    return jnp.where(condition, 1.0, 0.0)


def chip_places(x):
    return [lax.rem(x - d + 4, 4) for d in range(4)]


def between(totals, place, low, high):
    return sum(t * flag((low < p) & (p < high)) for t, p in zip(totals, place))


def row_key_kernel(pair, place_ref, sent_ref, chip_ref, r1, r2, r3, tie_ref, in_ref, whole_ref, table_ref, tied_ref):
    tied_ref[...] = tie_ref[...]
    x = place_ref[2]
    n = pair * DH
    refs = (sent_ref, r1, r2, r3)
    place = chip_places(x)
    tails = [ref[pl.ds(n, 16), :] for ref in refs]
    for j in range(pair):
        totals = [total_in(tail, j) for tail in tails]
        at = pl.ds(j * DH, DH)
        inside = 0.0
        whole = jnp.exp(between(totals, place, x, 4)) * chip_ref[at, :]
        for d in range(1, 4):
            state = refs[d][at, :].astype(jnp.float32)
            whole += jnp.exp(between(totals, place, place[d], 4)) * state
            inside += jnp.exp(between(totals, place, place[d], x)) * flag(place[d] < x) * state
        in_ref[at, :] = inside
        whole_ref[at, :] = whole
        lines = totals + [
            jnp.exp(between(totals, place, -1, x)), jnp.exp(between(totals, place, x, 4)), sum(totals), jnp.zeros_like(totals[0])
        ]
        for i, line in enumerate(lines):
            table_ref[pl.ds(8 * j + i, 1), :] = line


def row_grad_kernel(pair, place_ref, chip_ref, r1, r2, r3, whole_key, table_ref, tie_ref, in_ref, s1, s2, s3, tied_ref):
    x, y = place_ref[2], place_ref[3]
    n = pair * DH
    refs = (chip_ref, r1, r2, r3)
    place = chip_places(x)
    row_totals = []
    for j in range(pair):
        totals = [table_ref[pl.ds(8 * j + d, 1), :] for d in range(4)]
        row_totals.append(table_ref[pl.ds(8 * j + 6, 1), :])
        at = pl.ds(j * DH, DH)
        inside = 0.0
        whole = jnp.exp(between(totals, place, -1, x)) * chip_ref[at, :]
        for d in range(1, 4):
            state = refs[d][at, :].astype(jnp.float32)
            whole += jnp.exp(between(totals, place, -1, place[d])) * state
            inside += jnp.exp(between(totals, place, x, place[d])) * flag(place[d] > x) * state
        in_ref[at, :] = inside
        for dy, ref in ((1, s1), (2, s2), (3, s3)):
            ref[at, :] = jnp.where(y + dy < 4, whole_key[at, :], whole).astype(jnp.bfloat16)
    tail = tail_of(row_totals)
    for ref in (s1, s2, s3):
        ref[pl.ds(n, 16), :] = tail
    tied_ref[...] = tie_ref[...]


def enter_kernel(pair, place_ref, key_in, grad_in, table_ref, r1, r2, r3, tie_ref, enter_ref, tied_ref):
    tied_ref[...] = tie_ref[...]
    y = place_ref[3]
    n = pair * DH
    refs = (r1, r2, r3)
    place = [lax.rem(y - d + 4, 4) for d in (1, 2, 3)]
    tails = [ref[pl.ds(n, 16), :] for ref in refs]
    for j in range(pair):
        totals = [total_in(tail, j) for tail in tails]
        at = pl.ds(j * DH, DH)
        key, grad = key_in[at, :], grad_in[at, :]
        into, out = table_ref[pl.ds(8 * j + 4, 1), :], table_ref[pl.ds(8 * j + 5, 1), :]
        for d in range(3):
            p = place[d]
            gap = sum(t * flag(((p < q) & (q < y)) | ((y < q) & (q < p))) for t, q in zip(totals, place))
            weight = jnp.exp(gap)
            state = refs[d][at, :].astype(jnp.float32)
            key += into * weight * flag(p < y) * state
            grad += out * weight * flag(p > y) * state
        enter_ref[at, :] = key
        enter_ref[pl.ds((pair + j) * DH, DH), :] = grad


def close_kernel(heads, place_ref, enter_ref, enter_other, key_other, grad_other, ga_ref, k_ref, v_ref, *refs):
    halves, outs, room, sems = (refs[:5], refs[5:10]), refs[10:13], refs[13], refs[14]
    core = place_ref[1]
    pair = heads // 2
    first = core == 0
    copies = []

    def fold(x):
        return x[:, :DH] + x[:, DH:]

    for h in range(heads):
        start_w, end_w, dq, dk, dv = halves[h // pair]
        i = h % pair
        at, low = pl.ds(i * DH, DH), pl.ds((pair + i) * DH, DH)
        cols, mine = slice(h * DH, (h + 1) * DH), slice(i * DH, (i + 1) * DH)
        here = core == h // pair
        key = jnp.where(here, enter_ref[at, :], enter_other[at, :])
        grad = jnp.where(here, enter_ref[low, :], enter_other[low, :])
        decay = jnp.exp(key_other[pl.ds(heads * DH + h, 1), :])
        si = jnp.where(first, key, decay * key + key_other[pl.ds(h * DH, DH), :])
        so = jnp.where(first, decay * grad + grad_other[pl.ds(h * DH, DH), :], grad)
        si = jnp.concatenate(pieces(si, 2), axis=0)
        hi, lo = pieces(so, 2)
        so = jnp.concatenate([hi, lo], axis=0)
        so_wide = jnp.concatenate([hi, lo], axis=1)
        room[0, h] = dq[:, mine] + start_w[:, mine] * fold(dot(ga_ref[:, cols], si, NT))
        room[1, h] = dk[:, mine] + end_w[:, mine] * fold(dot(v_ref[:, cols], so, NT))
        room[2, h] = dv[:, mine] + end_w[:, mine] * fold(dot(k_ref[:, cols], so_wide, NN))
        for j in range(3):
            copy = pltpu.make_async_copy(room.at[j, h], outs[j].at[:, pl.ds(h * DH, DH)], sems.at[j, h])
            copy.start()
            copies.append(copy)
    for copy in copies:
        copy.wait()


def local(queries, keys, values, log_decay, out_weight, grad_out):
    rows, width = queries.shape
    heads = log_decay.shape[0]
    pair = heads // 2
    z = lax.axis_index("head")
    seq = lax.axis_index("seq")
    place = jnp.stack([z, seq % 2, (seq // 2) % 4, seq // 8]).astype(jnp.int32)

    def along_z(array):
        pairs = []
        for i in range(32):
            for j in range(8):
                pairs.append((i * 8 + j, i * 8 + (j + (1 if i % 2 == 0 else -1)) % 8))
        return lax.ppermute(array, ("seq", "head"), pairs)

    def along_seq(array, dy=0, dx=0, flip=False):
        pairs = []
        for i in range(32):
            a, b, c = i // 8, (i // 2) % 4, i % 2
            pairs.append((i, ((a + dy) % 4) * 8 + ((b + dx) % 4) * 2 + (1 - c if flip else c)))
        return lax.ppermute(array, "seq", pairs)

    def other(array):
        return along_seq(array, flip=True)

    def in_hbm(array):
        return pltpu.with_memory_space_constraint(array, pltpu.HBM)

    b0 = other(grad_out)
    key_own, b0 = call(
        functools.partial(open_kernel, heads), (f32(heads * DH + 8, DH), bf16(*grad_out.shape)),
        in_hbm(keys), in_hbm(values), log_decay, b0,
        specs=[ANY] * 2 + [VMEM] * 2,
        scratch=[pltpu.VMEM((rows, width), jnp.bfloat16)] * 2 + [pltpu.SemaphoreType.DMA((2,))],
    )
    a1 = along_z(grad_out)
    b1 = along_z(b0)

    key_other = other(key_own)
    sent, chip, a1 = call(
        functools.partial(chip_key_kernel, heads), (bf16(pair * DH + 16, DH), f32(pair * DH, DH), bf16(*grad_out.shape)),
        place, key_own, key_other, a1, specs=[SMEM] + [VMEM] * 3,
    )
    from_x = [along_seq(sent, dx=d) for d in (2, 1, 3)]
    from_x = [from_x[1], from_x[0], from_x[2]]
    a2 = along_z(a1)
    b1_here = other(b1)
    b2 = along_z(b1)
    key_in, key_row, table, a2 = call(
        functools.partial(row_key_kernel, pair),
        (f32(pair * DH, DH), f32(pair * DH, DH), f32(8 * pair, DH), bf16(*grad_out.shape)),
        place, sent, chip, *from_x, a2, specs=[SMEM] + [VMEM] * 6,
    )
    a3 = along_z(a2)
    b2_here = other(b2)
    b3 = along_z(b2)
    a4 = along_z(a3)
    b3_here = other(b3)

    qd = grad_out.shape[1]
    acc, w, qw, row, col = call(
        first_kernel,
        (f32(rows, width), bf16(3, width, qd), bf16(heads, 2 * DH, rows), f32(heads, rows), f32(rows, heads)),
        place, in_hbm(out_weight), in_hbm(grad_out), in_hbm(queries), log_decay, a1, b1_here, a2, b2_here,
        specs=[SMEM] + [ANY] * 3 + [VMEM] * 5,
        scratch=[
            pltpu.VMEM((5, width, qd), jnp.bfloat16), pltpu.VMEM((rows, qd), jnp.bfloat16),
            pltpu.VMEM((rows, width), jnp.bfloat16), pltpu.SemaphoreType.DMA((10,)),
        ],
    )
    (acc,) = call(second_kernel, (f32(rows, width),), acc, a3, b3_here, w)
    ga, grad_own = call(
        functools.partial(late_kernel, heads), (bf16(rows, width), f32(heads * DH, DH)), acc, a4, w, qw
    )

    grad_other = other(grad_own)
    sent, chip = call(
        functools.partial(chip_grad_kernel, heads), (bf16(pair * DH, DH), f32(pair * DH, DH)),
        place, key_own, key_other, grad_own, grad_other, specs=[SMEM] + [VMEM] * 4,
    )
    from_x = [along_seq(sent, dx=d) for d in (2, 1, 3)]
    from_x = [from_x[1], from_x[0], from_x[2]]
    def local_part(first):
        *parts, tie = call(
            functools.partial(local_kernel, pair, first), (f32(rows, pair * DH),) * 5 + (f32(8, DH),),
            queries, keys, values, ga, row, col,
        )
        dq, dk, dv, start_w, end_w = parts
        return (start_w, end_w, dq, dk, dv), tie

    low, tie = local_part(0)
    high, tie_high = local_part(pair)
    grad_in, *sent, _ = call(
        functools.partial(row_grad_kernel, pair),
        (f32(pair * DH, DH),) + (bf16(pair * DH + 16, DH),) * 3 + (f32(8, DH),),
        place, chip, *from_x, key_row, table, tie, specs=[SMEM] + [VMEM] * 7,
    )
    from_y = [along_seq(sent[d - 1], dy=d) for d in (2, 1, 3)]
    from_y = [from_y[1], from_y[0], from_y[2]]
    enter, _ = call(
        functools.partial(enter_kernel, pair), (f32(2 * pair * DH, DH), f32(8, DH)),
        place, key_in, grad_in, table, *from_y, tie_high, specs=[SMEM] + [VMEM] * 7,
    )
    enter_other = other(enter)

    return pl.pallas_call(
        functools.partial(close_kernel, heads),
        out_shape=(f32(rows, width),) * 3,
        in_specs=[SMEM] + [VMEM] * 17,
        out_specs=(ANY,) * 3,
        scratch_shapes=[pltpu.VMEM((3, heads, rows, DH), jnp.float32), pltpu.SemaphoreType.DMA((3, heads))],
        compiler_params=pltpu.CompilerParams(vmem_limit_bytes=24 * 2**20),
    )(place, enter, enter_other, key_other, grad_other, ga, keys, values, *low, *high)


def solution(mesh):
    return jax.shard_map(
        local,
        mesh=mesh,
        in_specs=(
            P("seq", "head"),
            P("seq", "head"),
            P("seq", "head"),
            P("head", "seq"),
            P("head", None),
            P("seq", "head"),
        ),
        out_specs=(P("seq", "head"), P("seq", "head"), P("seq", "head")),
        check_vma=False,
    )
```

```python
import functools

import jax
import jax.numpy as jnp
from jax import lax
from jax.experimental import pallas as pl
from jax.experimental.pallas import tpu as pltpu
from jax.sharding import PartitionSpec as P

DH = 128
NT = (((1,), (1,)), ((), ()))
NN = (((1,), (0,)), ((), ()))
TN = (((0,), (0,)), ((), ()))
VMEM = pl.BlockSpec(memory_space=pltpu.VMEM)
ANY = pl.BlockSpec(memory_space=pl.ANY)


def dot(a, b, dims):
    return lax.dot_general(a, b, dims, preferred_element_type=jnp.float32)


def pieces(x, n):
    out = []
    for _ in range(n):
        p = x.astype(jnp.bfloat16)
        out.append(p)
        x = x - p.astype(jnp.float32)
    return out


def call(kernel, outs, *args, specs=None, limit=24, scratch=(), aliases=None):
    return pl.pallas_call(
        kernel,
        out_shape=outs,
        in_specs=specs or [VMEM] * len(args),
        out_specs=tuple(VMEM for _ in outs),
        scratch_shapes=scratch,
        input_output_aliases=aliases or {},
        compiler_params=pltpu.CompilerParams(vmem_limit_bytes=limit * 2**20),
    )(*args)


def f32(*shape):
    return jax.ShapeDtypeStruct(shape, jnp.float32)


def bf16(*shape):
    return jax.ShapeDtypeStruct(shape, jnp.bfloat16)


def running(ld):
    n = ld.shape[1]
    s = lax.broadcasted_iota(jnp.int32, (n, n), 0)
    t = lax.broadcasted_iota(jnp.int32, (n, n), 1)
    upto = jnp.where(s <= t, 1.0, 0.0).astype(jnp.bfloat16)
    parts = pieces(ld, 3)
    return sum(dot(p, upto, NN) for p in parts), sum(dot(p, jnp.ones((n, DH), jnp.bfloat16), NN) for p in parts)


def running_columns(ld):
    n = ld.shape[1]
    s = lax.broadcasted_iota(jnp.int32, (n, n), 0)
    t = lax.broadcasted_iota(jnp.int32, (n, n), 1)
    since = jnp.where(s >= t, 1.0, 0.0).astype(jnp.bfloat16)
    return sum(dot(since, p, NT) for p in pieces(ld, 3))


def open_kernel(heads, k_hbm, v_hbm, ld_ref, tie_ref, state_ref, tied_ref, k_ref, v_ref, sems):
    copies = [pltpu.make_async_copy(src, dst, sems.at[i]) for i, (src, dst) in enumerate(((k_hbm, k_ref), (v_hbm, v_ref)))]
    for copy in copies:
        copy.start()
    tied_ref[...] = tie_ref[...]
    n = k_ref.shape[0]
    row, total = running(ld_ref[...])
    state_ref[pl.ds(heads * DH, heads), :] = total
    state_ref[pl.ds(heads * DH + heads, 8 - heads), :] = jnp.zeros((8 - heads, DH), jnp.float32)
    for copy in copies:
        copy.wait()
    for h in range(heads):
        cols = slice(h * DH, (h + 1) * DH)
        kt = k_ref[:, cols].T.astype(jnp.float32) * jnp.exp(row[h : h + 1, n - 1 : n] - row[h : h + 1, :])
        hi, lo = pieces(kt, 2)
        v = v_ref[:, cols]
        state_ref[pl.ds(h * DH, DH), :] = dot(hi, v, NN) + dot(lo, v, NN)


def local_kernel(heads, first, q_ref, k_ref, v_ref, ga_ref, row_ref, col_ref, dq_ref, dk_ref, dv_ref, start_ref, end_ref, tie_ref):
    n = q_ref.shape[0]
    step = n // 2
    s = lax.broadcasted_iota(jnp.int32, (step, step), 0)
    t = lax.broadcasted_iota(jnp.int32, (step, step), 1)
    keep = s <= t
    for i in range(heads):
        h = first + i
        cols, to = slice(h * DH, (h + 1) * DH), slice(i * DH, (i + 1) * DH)
        col = col_ref[:, h : h + 1]
        start_ref[:, to] = jnp.broadcast_to(jnp.exp(col) * (1.0 / DH), (n, DH))
        end_ref[:, to] = jnp.broadcast_to(jnp.exp(row_ref[h : h + 1, n - 1 : n] - col) * (1.0 / DH), (n, DH))
        for sb in range(2):
            srows = slice(sb * step, (sb + 1) * step)
            k, v = k_ref[srows, cols], v_ref[srows, cols]
            col = col_ref[srows, h : h + 1]
            dk = dv = None
            for tb in range(sb, 2):
                trows = slice(tb * step, (tb + 1) * step)
                q, ga = q_ref[trows, cols], ga_ref[trows, cols]
                gap = row_ref[h : h + 1, trows] - col
                if tb == sb:
                    gap = jnp.where(keep, gap, -jnp.inf)
                weight = jnp.exp(gap) * (1.0 / DH)
                scores = (dot(k, q, NT) * weight).astype(jnp.bfloat16)
                grads = (dot(v, ga, NT) * weight).astype(jnp.bfloat16)
                dv_part = dot(scores, ga, NN)
                dk_part = dot(grads, q, NN)
                dv = dv_part if dv is None else dv + dv_part
                dk = dk_part if dk is None else dk + dk_part
                dq = dot(grads, k, TN)
                if sb == 0:
                    dq_ref[trows, to] = dq
                else:
                    dq_ref[trows, to] += dq
            dk_ref[srows, to] = dk
            dv_ref[srows, to] = dv
    tie_ref[...] = jnp.zeros(tie_ref.shape, jnp.float32)


def first_kernel(
    w_hbm, c_hbm, q_hbm, ld_ref, a1, b1, a2, b2, a3,
    acc_ref, w_ref, qw_ref, row_ref, col_ref, near_ref, c_ref, q_ref, sems,
):
    z, side = lax.axis_index("head"), 1 - 2 * core_index()
    rows, width = c_ref.shape
    heads = ld_ref.shape[0]
    targets = [near_ref.at[i] for i in range(6)] + [w_ref.at[i] for i in range(2)]
    copies = [pltpu.make_async_copy(c_hbm, c_ref, sems.at[8]), pltpu.make_async_copy(q_hbm, q_ref, sems.at[9])]
    for i, (offset, target) in enumerate(zip((0, -1, 1, -2, 2, -3, 4, 3), targets)):
        at = lax.rem(z + offset * side + 8, 8) * width
        copies.append(pltpu.make_async_copy(w_hbm.at[:, pl.ds(pl.multiple_of(at, 128), width)], target, sems.at[i]))
    for copy in copies:
        copy.start()
    row, _ = running(ld_ref[...])
    row_ref[...] = row
    col_ref[...] = running_columns(ld_ref[...])
    copies[1].wait()
    for h in range(heads):
        qt = q_ref[:, h * DH : (h + 1) * DH].T.astype(jnp.float32) * jnp.exp(row[h : h + 1, :])
        hi, lo = pieces(qt, 2)
        qw_ref[h, :DH, :] = hi
        qw_ref[h, DH:, :] = lo
    copies[0].wait()
    for copy in copies[2:]:
        copy.wait()
    half = rows // 2
    for part in range(2):
        at = pl.ds(part * half, half)
        acc = dot(c_ref[at, :], near_ref[0], NT)
        for i, ref in enumerate((a1, b1, a2, b2, a3)):
            acc += dot(ref[at, :], near_ref[i + 1], NT)
        acc_ref[at, :] = acc


def second_kernel(acc_ref, a4, w_ref, out_ref):
    half = acc_ref.shape[0] // 2
    for part in range(2):
        at = pl.ds(part * half, half)
        out_ref[at, :] = acc_ref[at, :] + dot(a4[at, :], w_ref[0], NT)


def late_kernel(heads, acc_ref, a4, b3, w_ref, qw_ref, ga_ref, state_ref):
    half = acc_ref.shape[0] // 2
    for part in range(2):
        at = pl.ds(part * half, half)
        ga_ref[at, :] = (
            acc_ref[at, :] + dot(a4[at, :], w_ref[0], NT) + dot(b3[at, :], w_ref[1], NT)
        ).astype(jnp.bfloat16)
    for h in range(heads):
        both = dot(qw_ref[h], ga_ref[:, h * DH : (h + 1) * DH], NN)
        state_ref[pl.ds(h * DH, DH), :] = both[:DH] + both[DH:]


def gate_kernel(x_ref, tie_ref, out_ref):
    out_ref[...] = x_ref[...]


def core_index():
    return lax.rem(lax.axis_index("seq"), 2)


def x_index():
    return lax.rem(lax.div(lax.axis_index("seq"), 2), 4)


def y_index():
    return lax.div(lax.axis_index("seq"), 8)


def one_row(tile, i):
    return jnp.sum(jnp.where(lax.broadcasted_iota(jnp.int32, tile.shape, 0) == i, tile, 0.0), axis=0, keepdims=True)


def tail_of(totals):
    parts = [[p.astype(jnp.float32) for p in pieces(t, 3)] for t in totals]
    at = lax.broadcasted_iota(jnp.int32, (16, DH), 0)
    out = jnp.zeros((16, DH), jnp.float32)
    for j, three in enumerate(parts):
        for i, part in enumerate(three):
            out = jnp.where(at == 3 * j + i, part, out)
    return out.astype(jnp.bfloat16)


def total_in(tail, j):
    tail = tail.astype(jnp.float32)
    return one_row(tail, 3 * j) + one_row(tail, 3 * j + 1) + one_row(tail, 3 * j + 2)


def chip_key_kernel(heads, key_ref, key_other, tie_ref, sent_ref, chip_ref, tied_ref):
    tied_ref[...] = tie_ref[...]
    core = core_index()
    pair = heads // 2
    first = core == 0
    totals = []
    for j in range(pair):
        h = core * pair + j
        mine = one_row(key_ref[heads * DH :, :], h)
        others = one_row(key_other[heads * DH :, :], h)
        totals.append(mine + others)
        at = pl.ds(pl.multiple_of(h * DH, DH), DH)
        key = jnp.where(first, jnp.exp(others), 1.0) * key_ref[at, :] + jnp.where(first, 1.0, jnp.exp(mine)) * key_other[at, :]
        chip_ref[pl.ds(j * DH, DH), :] = key
        sent_ref[pl.ds(j * DH, DH), :] = key.astype(jnp.bfloat16)
    sent_ref[pl.ds(pair * DH, 16), :] = tail_of(totals)


def chip_grad_kernel(heads, key_ref, key_other, grad_ref, grad_other, sent_ref, chip_ref):
    core = core_index()
    pair = heads // 2
    first = core == 0
    for j in range(pair):
        h = core * pair + j
        mine = jnp.exp(one_row(key_ref[heads * DH :, :], h))
        others = jnp.exp(one_row(key_other[heads * DH :, :], h))
        at = pl.ds(pl.multiple_of(h * DH, DH), DH)
        grad = jnp.where(first, 1.0, others) * grad_ref[at, :] + jnp.where(first, mine, 1.0) * grad_other[at, :]
        chip_ref[pl.ds(j * DH, DH), :] = grad
        sent_ref[pl.ds(j * DH, DH), :] = grad.astype(jnp.bfloat16)


def flag(condition):
    return jnp.where(condition, 1.0, 0.0)


def chip_places(x):
    return [lax.rem(x - d + 4, 4) for d in range(4)]


def between(totals, place, low, high):
    return sum(t * flag((low < p) & (p < high)) for t, p in zip(totals, place))


def row_key_kernel(pair, sent_ref, chip_ref, r1, r2, r3, tie_ref, in_ref, whole_ref, table_ref, tail_ref, tied_ref):
    tied_ref[...] = tie_ref[...]
    x = x_index()
    n = pair * DH
    refs = (sent_ref, r1, r2, r3)
    place = chip_places(x)
    tails = [ref[pl.ds(n, 16), :] for ref in refs]
    row_totals = []
    for j in range(pair):
        totals = [total_in(tail, j) for tail in tails]
        at = pl.ds(j * DH, DH)
        inside = 0.0
        whole = jnp.exp(between(totals, place, x, 4)) * chip_ref[at, :]
        for d in range(1, 4):
            state = refs[d][at, :].astype(jnp.float32)
            whole += jnp.exp(between(totals, place, place[d], 4)) * state
            inside += jnp.exp(between(totals, place, place[d], x)) * flag(place[d] < x) * state
        in_ref[at, :] = inside
        whole_ref[at, :] = whole
        lines = [jnp.exp(between(totals, place, -1, p)) for p in place]
        lines += [jnp.exp(between(totals, place, x, p)) * flag(p > x) for p in place[1:]]
        lines += [jnp.exp(between(totals, place, -1, x)), jnp.exp(between(totals, place, x, 4))]
        for i, line in enumerate(lines):
            table_ref[pl.ds(16 * j + i, 1), :] = line
        table_ref[pl.ds(16 * j + 9, 7), :] = jnp.zeros((7, DH), jnp.float32)
        row_totals.append(sum(totals))
    tail_ref[...] = tail_of(row_totals)


def row_grad_kernel(pair, chip_ref, r1, r2, r3, whole_key, table_ref, tail_ref, _, in_ref, s1, s2, s3):
    y = y_index()
    n = pair * DH
    refs = (r1, r2, r3)

    def line(j, i):
        return table_ref[pl.ds(16 * j + i, 1), :]

    for j in range(pair):
        at = pl.ds(j * DH, DH)
        inside = 0.0
        whole = line(j, 0) * chip_ref[at, :]
        for d in range(3):
            state = refs[d][at, :].astype(jnp.float32)
            whole += line(j, 1 + d) * state
            inside += line(j, 4 + d) * state
        in_ref[at, :] = inside
        for dy, ref in ((1, s1), (2, s2), (3, s3)):
            ref[at, :] = jnp.where(y + dy < 4, whole_key[at, :], whole).astype(jnp.bfloat16)
    for ref in (s1, s2, s3):
        ref[pl.ds(n, 16), :] = tail_ref[...]


def enter_kernel(pair, key_in, grad_in, table_ref, r1, r2, r3, _, enter_ref):
    y = y_index()
    n = pair * DH
    refs = (r1, r2, r3)
    place = [lax.rem(y - d + 4, 4) for d in (1, 2, 3)]
    tails = [ref[pl.ds(n, 16), :] for ref in refs]
    for j in range(pair):
        totals = [total_in(tail, j) for tail in tails]
        at = pl.ds(j * DH, DH)
        key, grad = key_in[at, :], grad_in[at, :]
        into, out = table_ref[pl.ds(16 * j + 7, 1), :], table_ref[pl.ds(16 * j + 8, 1), :]
        for d in range(3):
            p = place[d]
            gap = sum(t * flag(((p < q) & (q < y)) | ((y < q) & (q < p))) for t, q in zip(totals, place))
            weight = jnp.exp(gap)
            state = refs[d][at, :].astype(jnp.float32)
            key += into * weight * flag(p < y) * state
            grad += out * weight * flag(p > y) * state
        enter_ref[at, :] = key
        enter_ref[pl.ds((pair + j) * DH, DH), :] = grad


def close_kernel(heads, enter_ref, enter_other, key_other, grad_other, ga_ref, k_ref, v_ref, *refs):
    halves, outs, room, sems = (refs[:5], refs[5:10]), refs[10:13], refs[13], refs[14]
    core = core_index()
    pair = heads // 2
    first = core == 0
    copies = []

    def fold(x):
        return x[:, :DH] + x[:, DH:]

    for h in range(heads):
        start_w, end_w, dq, dk, dv = halves[h // pair]
        i = h % pair
        at, low = pl.ds(i * DH, DH), pl.ds((pair + i) * DH, DH)
        cols, mine = slice(h * DH, (h + 1) * DH), slice(i * DH, (i + 1) * DH)
        here = core == h // pair
        key = jnp.where(here, enter_ref[at, :], enter_other[at, :])
        grad = jnp.where(here, enter_ref[low, :], enter_other[low, :])
        decay = jnp.exp(key_other[pl.ds(heads * DH + h, 1), :])
        si = jnp.where(first, key, decay * key + key_other[pl.ds(h * DH, DH), :])
        so = jnp.where(first, decay * grad + grad_other[pl.ds(h * DH, DH), :], grad)
        si = jnp.concatenate(pieces(si, 2), axis=0)
        hi, lo = pieces(so, 2)
        so = jnp.concatenate([hi, lo], axis=0)
        so_wide = jnp.concatenate([hi, lo], axis=1)
        for part in range(4):
            step = ga_ref.shape[0] // 4
            rows = pl.ds(part * step, step)
            room[0, h, rows] = dq[rows, mine] + start_w[rows, mine] * fold(dot(ga_ref[rows, cols], si, NT))
            room[1, h, rows] = dk[rows, mine] + end_w[rows, mine] * fold(dot(v_ref[rows, cols], so, NT))
            room[2, h, rows] = dv[rows, mine] + end_w[rows, mine] * fold(dot(k_ref[rows, cols], so_wide, NN))
            if part % 2:
                at = pl.ds((part - 1) * step, 2 * step)
                for j in range(3):
                    copy = pltpu.make_async_copy(
                        room.at[j, h, at], outs[j].at[at, pl.ds(h * DH, DH)], sems.at[j, 2 * h + part // 2]
                    )
                    copy.start()
                    copies.append(copy)
    for copy in copies:
        copy.wait()


def local(queries, keys, values, log_decay, out_weight, grad_out):
    rows, width = queries.shape
    heads = log_decay.shape[0]
    pair = heads // 2

    def along_z(array):
        pairs = []
        for i in range(32):
            for j in range(8):
                pairs.append((i * 8 + j, i * 8 + (j + (1 if i % 2 == 0 else -1)) % 8))
        return lax.ppermute(array, ("seq", "head"), pairs)

    def along_seq(array, dy=0, dx=0, flip=False):
        pairs = []
        for i in range(32):
            a, b, c = i // 8, (i // 2) % 4, i % 2
            pairs.append((i, ((a + dy) % 4) * 8 + ((b + dx) % 4) * 2 + (1 - c if flip else c)))
        return lax.ppermute(array, "seq", pairs)

    def other(array):
        return along_seq(array, flip=True)

    def in_hbm(array):
        return pltpu.with_memory_space_constraint(array, pltpu.HBM)

    b0 = other(grad_out)
    key_own, b0 = call(
        functools.partial(open_kernel, heads), (f32(heads * DH + 8, DH), bf16(*grad_out.shape)),
        in_hbm(keys), in_hbm(values), log_decay, b0,
        specs=[ANY] * 2 + [VMEM] * 2,
        scratch=[pltpu.VMEM((rows, width), jnp.bfloat16)] * 2 + [pltpu.SemaphoreType.DMA((2,))],
    )
    a1 = along_z(grad_out)
    b1 = along_z(b0)

    key_other = other(key_own)
    sent, chip, a1 = call(
        functools.partial(chip_key_kernel, heads), (bf16(pair * DH + 16, DH), f32(pair * DH, DH), bf16(*grad_out.shape)),
        key_own, key_other, a1, specs=[VMEM] * 3,
    )
    from_x = [along_seq(sent, dx=d) for d in (2, 1, 3)]
    from_x = [from_x[1], from_x[0], from_x[2]]
    a2 = along_z(a1)
    b1_here = other(b1)
    b2 = along_z(b1)
    b2_here = other(b2)
    key_in, key_row, table, tail, b2 = call(
        functools.partial(row_key_kernel, pair),
        (f32(pair * DH, DH), f32(pair * DH, DH), f32(16 * pair, DH), bf16(16, DH), bf16(*grad_out.shape)),
        sent, chip, *from_x, b2, specs=[VMEM] * 6,
    )
    a3 = along_z(a2)
    b3 = along_z(b2)
    a4 = along_z(a3)

    qd = grad_out.shape[1]
    acc, w, qw, row, col = call(
        first_kernel,
        (f32(rows, width), bf16(2, width, qd), bf16(heads, 2 * DH, rows), f32(heads, rows), f32(rows, heads)),
        in_hbm(out_weight), in_hbm(grad_out), in_hbm(queries), log_decay, a1, b1_here, a2, b2_here, a3,
        specs=[ANY] * 3 + [VMEM] * 6,
        scratch=[
            pltpu.VMEM((6, width, qd), jnp.bfloat16), pltpu.VMEM((rows, qd), jnp.bfloat16),
            pltpu.VMEM((rows, width), jnp.bfloat16), pltpu.SemaphoreType.DMA((10,)),
        ],
    )
    b3_here = other(call(gate_kernel, (bf16(*grad_out.shape),), b3, acc)[0])
    ga, grad_own = call(
        functools.partial(late_kernel, heads), (bf16(rows, width), f32(heads * DH, DH)), acc, a4, b3_here, w, qw
    )

    grad_other = other(grad_own)
    sent, chip = call(
        functools.partial(chip_grad_kernel, heads), (bf16(pair * DH, DH), f32(pair * DH, DH)),
        key_own, key_other, grad_own, grad_other, specs=[VMEM] * 4,
    )
    from_x = [along_seq(sent, dx=d) for d in (2, 1, 3)]
    from_x = [from_x[1], from_x[0], from_x[2]]
    def local_part(first):
        *parts, tie = call(
            functools.partial(local_kernel, pair, first), (f32(rows, pair * DH),) * 5 + (f32(8, DH),),
            queries, keys, values, ga, row, col,
        )
        dq, dk, dv, start_w, end_w = parts
        return (start_w, end_w, dq, dk, dv), tie

    low, tie = local_part(0)
    high, tie_high = local_part(pair)
    grad_in, *sent = call(
        functools.partial(row_grad_kernel, pair),
        (f32(pair * DH, DH),) + (bf16(pair * DH + 16, DH),) * 3,
        chip, *from_x, key_row, table, tail, tie, specs=[VMEM] * 8,
    )
    from_y = [along_seq(sent[d - 1], dy=d) for d in (2, 1, 3)]
    from_y = [from_y[1], from_y[0], from_y[2]]
    (enter,) = call(
        functools.partial(enter_kernel, pair), (f32(2 * pair * DH, DH),),
        key_in, grad_in, table, *from_y, tie_high, specs=[VMEM] * 7,
    )
    enter_other = other(enter)

    return pl.pallas_call(
        functools.partial(close_kernel, heads),
        out_shape=(f32(rows, width),) * 3,
        in_specs=[VMEM] * 17,
        out_specs=(ANY,) * 3,
        scratch_shapes=[pltpu.VMEM((3, heads, rows, DH), jnp.float32), pltpu.SemaphoreType.DMA((3, 2 * heads))],
        compiler_params=pltpu.CompilerParams(vmem_limit_bytes=24 * 2**20),
    )(enter, enter_other, key_other, grad_other, ga, keys, values, *low, *high)


def solution(mesh):
    return jax.shard_map(
        local,
        mesh=mesh,
        in_specs=(
            P("seq", "head"),
            P("seq", "head"),
            P("seq", "head"),
            P("head", "seq"),
            P("head", None),
            P("seq", "head"),
        ),
        out_specs=(P("seq", "head"), P("seq", "head"), P("seq", "head")),
        check_vma=False,
    )
```

```python
import functools

import jax
import jax.numpy as jnp
from jax import lax
from jax.experimental import pallas as pl
from jax.experimental.pallas import tpu as pltpu
from jax.sharding import PartitionSpec as P

DH = 128
NT = (((1,), (1,)), ((), ()))
NN = (((1,), (0,)), ((), ()))
TN = (((0,), (0,)), ((), ()))
VMEM = pl.BlockSpec(memory_space=pltpu.VMEM)
ANY = pl.BlockSpec(memory_space=pl.ANY)


def dot(a, b, dims):
    return lax.dot_general(a, b, dims, preferred_element_type=jnp.float32)


def pieces(x, n):
    out = []
    for _ in range(n):
        p = x.astype(jnp.bfloat16)
        out.append(p)
        x = x - p.astype(jnp.float32)
    return out


def call(kernel, outs, *args, specs=None, limit=24, scratch=(), aliases=None):
    return pl.pallas_call(
        kernel,
        out_shape=outs,
        in_specs=specs or [VMEM] * len(args),
        out_specs=tuple(VMEM for _ in outs),
        scratch_shapes=scratch,
        input_output_aliases=aliases or {},
        compiler_params=pltpu.CompilerParams(vmem_limit_bytes=limit * 2**20),
    )(*args)


def f32(*shape):
    return jax.ShapeDtypeStruct(shape, jnp.float32)


def bf16(*shape):
    return jax.ShapeDtypeStruct(shape, jnp.bfloat16)


def running(ld):
    n = ld.shape[1]
    s = lax.broadcasted_iota(jnp.int32, (n, n), 0)
    t = lax.broadcasted_iota(jnp.int32, (n, n), 1)
    upto = jnp.where(s <= t, 1.0, 0.0).astype(jnp.bfloat16)
    parts = pieces(ld, 3)
    return sum(dot(p, upto, NN) for p in parts), sum(dot(p, jnp.ones((n, DH), jnp.bfloat16), NN) for p in parts)


def running_columns(ld):
    n = ld.shape[1]
    s = lax.broadcasted_iota(jnp.int32, (n, n), 0)
    t = lax.broadcasted_iota(jnp.int32, (n, n), 1)
    since = jnp.where(s >= t, 1.0, 0.0).astype(jnp.bfloat16)
    return sum(dot(since, p, NT) for p in pieces(ld, 3))


def open_kernel(heads, k_hbm, v_hbm, ld_hbm, tie_ref, state_ref, tied_ref, k_ref, v_ref, ld_ref, sems):
    copies = [pltpu.make_async_copy(src, dst, sems.at[i]) for i, (src, dst) in enumerate(((ld_hbm, ld_ref), (k_hbm, k_ref), (v_hbm, v_ref)))]
    for copy in copies:
        copy.start()
    tied_ref[...] = tie_ref[...]
    n = k_ref.shape[0]
    copies[0].wait()
    row, total = running(ld_ref[...])
    state_ref[pl.ds(heads * DH, heads), :] = total
    state_ref[pl.ds(heads * DH + heads, 8 - heads), :] = jnp.zeros((8 - heads, DH), jnp.float32)
    for copy in copies[1:]:
        copy.wait()
    for h in range(heads):
        cols = slice(h * DH, (h + 1) * DH)
        kt = k_ref[:, cols].T.astype(jnp.float32) * jnp.exp(row[h : h + 1, n - 1 : n] - row[h : h + 1, :])
        hi, lo = pieces(kt, 2)
        v = v_ref[:, cols]
        state_ref[pl.ds(h * DH, DH), :] = dot(hi, v, NN) + dot(lo, v, NN)


def head_columns(position):
    return pl.ds(pl.multiple_of(lax.rem(core_index() * 2 + position, 4) * DH, DH), DH)


def local_kernel(heads, first, q_ref, k_ref, v_ref, ga_ref, row_ref, col_ref, dq_ref, dk_ref, dv_ref, start_ref, end_ref, tie_ref):
    n = q_ref.shape[0]
    step = n // 2
    s = lax.broadcasted_iota(jnp.int32, (step, step), 0)
    t = lax.broadcasted_iota(jnp.int32, (step, step), 1)
    keep = s <= t
    for i in range(heads):
        h = first + i
        cols, to = head_columns(h), slice(i * DH, (i + 1) * DH)
        col = col_ref[:, h : h + 1]
        start_ref[:, to] = jnp.broadcast_to(jnp.exp(col) * (1.0 / DH), (n, DH))
        end_ref[:, to] = jnp.broadcast_to(jnp.exp(row_ref[h : h + 1, n - 1 : n] - col) * (1.0 / DH), (n, DH))
        for sb in range(2):
            srows = slice(sb * step, (sb + 1) * step)
            k, v = k_ref[srows, cols], v_ref[srows, cols]
            col = col_ref[srows, h : h + 1]
            dk = dv = None
            for tb in range(sb, 2):
                trows = slice(tb * step, (tb + 1) * step)
                q, ga = q_ref[trows, cols], ga_ref[trows, cols]
                gap = row_ref[h : h + 1, trows] - col
                if tb == sb:
                    gap = jnp.where(keep, gap, -jnp.inf)
                weight = jnp.exp(gap) * (1.0 / DH)
                scores = (dot(k, q, NT) * weight).astype(jnp.bfloat16)
                grads = (dot(v, ga, NT) * weight).astype(jnp.bfloat16)
                dv_part = dot(scores, ga, NN)
                dk_part = dot(grads, q, NN)
                dv = dv_part if dv is None else dv + dv_part
                dk = dk_part if dk is None else dk + dk_part
                dq = dot(grads, k, TN)
                if sb == 0:
                    dq_ref[trows, to] = dq
                else:
                    dq_ref[trows, to] += dq
            dk_ref[srows, to] = dk
            dv_ref[srows, to] = dv
    tie_ref[...] = jnp.zeros(tie_ref.shape, jnp.float32)


def first_kernel(
    w_hbm, c_hbm, q_hbm, ld_hbm, a1, b1, a2, b2, a3,
    acc_ref, w_ref, qw_ref, row_ref, col_ref, near_ref, c_ref, q_ref, ld_ref, sems,
):
    z, side = lax.axis_index("head"), 1 - 2 * core_index()
    rows, width = c_ref.shape
    heads = ld_ref.shape[0]
    targets = [near_ref.at[i] for i in range(6)] + [w_ref.at[i] for i in range(2)]
    decays = pltpu.make_async_copy(ld_hbm, ld_ref, sems.at[10])
    decays.start()
    copies = [pltpu.make_async_copy(c_hbm, c_ref, sems.at[8]), pltpu.make_async_copy(q_hbm, q_ref, sems.at[9])]
    for i, (offset, target) in enumerate(zip((0, -1, 1, -2, 2, -3, 4, 3), targets)):
        at = lax.rem(z + offset * side + 8, 8) * width
        copies.append(pltpu.make_async_copy(w_hbm.at[:, pl.ds(pl.multiple_of(at, 128), width)], target, sems.at[i]))
    for copy in copies:
        copy.start()
    decays.wait()
    row, _ = running(ld_ref[...])
    col = running_columns(ld_ref[...])
    swap = core_index() == 1
    row_ref[...] = jnp.where(swap, jnp.concatenate([row[heads // 2 :], row[: heads // 2]], axis=0), row)
    col_ref[...] = jnp.where(swap, jnp.concatenate([col[:, heads // 2 :], col[:, : heads // 2]], axis=1), col)
    copies[1].wait()
    for h in range(heads):
        qt = q_ref[:, h * DH : (h + 1) * DH].T.astype(jnp.float32) * jnp.exp(row[h : h + 1, :])
        hi, lo = pieces(qt, 2)
        qw_ref[h, :DH, :] = hi
        qw_ref[h, DH:, :] = lo
    copies[0].wait()
    for copy in copies[2:]:
        copy.wait()
    half = rows // 2
    for part in range(2):
        at = pl.ds(part * half, half)
        acc = dot(c_ref[at, :], near_ref[0], NT)
        for i, ref in enumerate((a1, b1, a2, b2, a3)):
            acc += dot(ref[at, :], near_ref[i + 1], NT)
        acc_ref[at, :] = acc


def second_kernel(acc_ref, a4, w_ref, out_ref):
    half = acc_ref.shape[0] // 2
    for part in range(2):
        at = pl.ds(part * half, half)
        out_ref[at, :] = acc_ref[at, :] + dot(a4[at, :], w_ref[0], NT)


def late_kernel(heads, acc_ref, a4, b3, w_ref, qw_ref, ga_ref, state_ref):
    half = acc_ref.shape[0] // 2
    for part in range(2):
        at = pl.ds(part * half, half)
        ga_ref[at, :] = (
            acc_ref[at, :] + dot(a4[at, :], w_ref[0], NT) + dot(b3[at, :], w_ref[1], NT)
        ).astype(jnp.bfloat16)
    for h in range(heads):
        both = dot(qw_ref[h], ga_ref[:, h * DH : (h + 1) * DH], NN)
        state_ref[pl.ds(h * DH, DH), :] = both[:DH] + both[DH:]


def gate_kernel(x_ref, tie_ref, out_ref):
    out_ref[...] = x_ref[...]


def core_index():
    return lax.rem(lax.axis_index("seq"), 2)


def x_index():
    return lax.rem(lax.div(lax.axis_index("seq"), 2), 4)


def y_index():
    return lax.div(lax.axis_index("seq"), 8)


def one_row(tile, i):
    return jnp.sum(jnp.where(lax.broadcasted_iota(jnp.int32, tile.shape, 0) == i, tile, 0.0), axis=0, keepdims=True)


def tail_of(totals):
    parts = [[p.astype(jnp.float32) for p in pieces(t, 3)] for t in totals]
    at = lax.broadcasted_iota(jnp.int32, (16, DH), 0)
    out = jnp.zeros((16, DH), jnp.float32)
    for j, three in enumerate(parts):
        for i, part in enumerate(three):
            out = jnp.where(at == 3 * j + i, part, out)
    return out.astype(jnp.bfloat16)


def total_in(tail, j):
    tail = tail.astype(jnp.float32)
    return one_row(tail, 3 * j) + one_row(tail, 3 * j + 1) + one_row(tail, 3 * j + 2)


def chip_key_kernel(heads, key_ref, key_other, tie_ref, sent_ref, chip_ref, tied_ref):
    tied_ref[...] = tie_ref[...]
    core = core_index()
    pair = heads // 2
    first = core == 0
    totals = []
    for j in range(pair):
        h = core * pair + j
        mine = one_row(key_ref[heads * DH :, :], h)
        others = one_row(key_other[heads * DH :, :], h)
        totals.append(mine + others)
        at = pl.ds(pl.multiple_of(h * DH, DH), DH)
        key = jnp.where(first, jnp.exp(others), 1.0) * key_ref[at, :] + jnp.where(first, 1.0, jnp.exp(mine)) * key_other[at, :]
        chip_ref[pl.ds(j * DH, DH), :] = key
        sent_ref[pl.ds(j * DH, DH), :] = key.astype(jnp.bfloat16)
    sent_ref[pl.ds(pair * DH, 16), :] = tail_of(totals)


def chip_grad_kernel(heads, key_ref, key_other, grad_ref, grad_other, sent_ref, chip_ref):
    core = core_index()
    pair = heads // 2
    first = core == 0
    for j in range(pair):
        h = core * pair + j
        mine = jnp.exp(one_row(key_ref[heads * DH :, :], h))
        others = jnp.exp(one_row(key_other[heads * DH :, :], h))
        at = pl.ds(pl.multiple_of(h * DH, DH), DH)
        grad = jnp.where(first, 1.0, others) * grad_ref[at, :] + jnp.where(first, mine, 1.0) * grad_other[at, :]
        chip_ref[pl.ds(j * DH, DH), :] = grad
        sent_ref[pl.ds(j * DH, DH), :] = grad.astype(jnp.bfloat16)


def flag(condition):
    return jnp.where(condition, 1.0, 0.0)


def places(x):
    return [jnp.bitwise_xor(x, d) for d in range(4)]


def between(totals, place, low, high):
    return sum(t * flag((low < p) & (p < high)) for t, p in zip(totals, place))


def row_key_kernel(pair, sent_ref, chip_ref, r1, r2, r3, tie_ref, in_ref, whole_ref, table_ref, tail_ref, tied_ref):
    tied_ref[...] = tie_ref[...]
    x = x_index()
    n = pair * DH
    refs = (sent_ref, r1, r2, r3)
    place = places(x)
    tails = [ref[pl.ds(n, 16), :] for ref in refs]
    row_totals = []
    for j in range(pair):
        totals = [total_in(tail, j) for tail in tails]
        at = pl.ds(j * DH, DH)
        inside = 0.0
        whole = jnp.exp(between(totals, place, x, 4)) * chip_ref[at, :]
        for d in range(1, 4):
            state = refs[d][at, :].astype(jnp.float32)
            whole += jnp.exp(between(totals, place, place[d], 4)) * state
            inside += jnp.exp(between(totals, place, place[d], x)) * flag(place[d] < x) * state
        in_ref[at, :] = inside
        whole_ref[at, :] = whole
        lines = [jnp.exp(between(totals, place, -1, p)) for p in place]
        lines += [jnp.exp(between(totals, place, x, p)) * flag(p > x) for p in place[1:]]
        lines += [jnp.exp(between(totals, place, -1, x)), jnp.exp(between(totals, place, x, 4))]
        for i, line in enumerate(lines):
            table_ref[pl.ds(16 * j + i, 1), :] = line
        table_ref[pl.ds(16 * j + 9, 7), :] = jnp.zeros((7, DH), jnp.float32)
        row_totals.append(sum(totals))
    tail_ref[...] = tail_of(row_totals)


def row_grad_kernel(pair, chip_ref, r1, r3, r2, whole_key, table_ref, tail_ref, _, in_ref, s1, s2, s3):
    y = y_index()
    n = pair * DH
    refs = (r1, r2, r3)

    def line(j, i):
        return table_ref[pl.ds(16 * j + i, 1), :]

    for j in range(pair):
        at = pl.ds(j * DH, DH)
        inside = 0.0
        whole = line(j, 0) * chip_ref[at, :]
        for d in range(3):
            state = refs[d][at, :].astype(jnp.float32)
            whole += line(j, 1 + d) * state
            inside += line(j, 4 + d) * state
        in_ref[at, :] = inside
        for dy, ref in ((1, s1), (2, s2), (3, s3)):
            ref[at, :] = jnp.where(jnp.bitwise_xor(y, dy) > y, whole_key[at, :], whole).astype(jnp.bfloat16)
    for ref in (s1, s2, s3):
        ref[pl.ds(n, 16), :] = tail_ref[...]


def enter_kernel(pair, key_in, grad_in, table_ref, r2, r1, r3, _, enter_ref):
    y = y_index()
    n = pair * DH
    refs = (r1, r2, r3)
    place = places(y)[1:]
    tails = [ref[pl.ds(n, 16), :] for ref in refs]
    for j in range(pair):
        totals = [total_in(tail, j) for tail in tails]
        at = pl.ds(j * DH, DH)
        key, grad = key_in[at, :], grad_in[at, :]
        into, out = table_ref[pl.ds(16 * j + 7, 1), :], table_ref[pl.ds(16 * j + 8, 1), :]
        for d in range(3):
            p = place[d]
            gap = sum(t * flag(((p < q) & (q < y)) | ((y < q) & (q < p))) for t, q in zip(totals, place))
            weight = jnp.exp(gap)
            state = refs[d][at, :].astype(jnp.float32)
            key += into * weight * flag(p < y) * state
            grad += out * weight * flag(p > y) * state
        enter_ref[at, :] = key
        enter_ref[pl.ds((pair + j) * DH, DH), :] = grad


def closed(first, i, part, enter_ref, key_other, grad_other, ga_ref, k_ref, v_ref, start_w, end_w, dq, dk, dv, states):
    core = core_index()
    heads = key_other.shape[0] // DH
    pair = heads // 2
    cols = head_columns(first + i)
    if i not in states:
        h = lax.rem(core * pair + first + i, heads)
        key = enter_ref[pl.ds(i * DH, DH), :]
        grad = enter_ref[pl.ds((pair + i) * DH, DH), :]
        decay = jnp.exp(one_row(key_other[heads * DH :, :], h))
        si = jnp.where(core == 0, key, decay * key + key_other[cols, :])
        so = jnp.where(core == 0, decay * grad + grad_other[cols, :], grad)
        hi, lo = pieces(so, 2)
        states[i] = jnp.concatenate(pieces(si, 2), axis=0), jnp.concatenate([hi, lo], axis=0), jnp.concatenate([hi, lo], axis=1)
    si, so, so_wide = states[i]
    mine = slice(i * DH, (i + 1) * DH)
    step = ga_ref.shape[0] // 4
    rows = pl.ds(part * step, step)

    def fold(x):
        return x[:, :DH] + x[:, DH:]

    return (
        dq[rows, mine] + start_w[rows, mine] * fold(dot(ga_ref[rows, cols], si, NT)),
        dk[rows, mine] + end_w[rows, mine] * fold(dot(v_ref[rows, cols], so, NT)),
        dv[rows, mine] + end_w[rows, mine] * fold(dot(k_ref[rows, cols], so_wide, NN)),
    )


def own_kernel(first, *refs):
    *inputs, out_ref = refs
    step = out_ref.shape[2] // 4
    states = {}
    for i in range(out_ref.shape[1]):
        for part in range(4):
            for j, value in enumerate(closed(first, i, part, *inputs, states)):
                out_ref[j, i, pl.ds(part * step, step)] = value


def rest_kernel(first, *refs):
    *inputs, own_ref, gq_ref, gk_ref, gv_ref, room, sems = refs
    outs = (gq_ref, gk_ref, gv_ref)
    pair, n = own_ref.shape[1:3]
    step = n // 4
    copies = []

    def send(src, j, position, at, sem):
        copy = pltpu.make_async_copy(src, outs[j].at[at, head_columns(position)], sem)
        copy.start()
        copies.append(copy)

    for i in range(pair):
        for j in range(3):
            send(own_ref.at[j, i], j, i, pl.ds(0, n), sems.at[j, i])
    states = {}
    for i in range(pair):
        for part in range(4):
            for j, value in enumerate(closed(first, i, part, *inputs, states)):
                room[j, i, pl.ds(part * step, step)] = value
            if part % 2:
                at = pl.ds((part - 1) * step, 2 * step)
                for j in range(3):
                    send(room.at[j, i, at], j, first + i, at, sems.at[j, pair + 2 * i + part // 2])
    for copy in copies:
        copy.wait()


def local(queries, keys, values, log_decay, out_weight, grad_out):
    rows, width = queries.shape
    heads = log_decay.shape[0]
    pair = heads // 2

    def along_z(array):
        pairs = []
        for i in range(32):
            for j in range(8):
                pairs.append((i * 8 + j, i * 8 + (j + (1 if i % 2 == 0 else -1)) % 8))
        return lax.ppermute(array, ("seq", "head"), pairs)

    def along_seq(array, dy=0, dx=0, flip=False):
        pairs = []
        for i in range(32):
            a, b, c = i // 8, (i // 2) % 4, i % 2
            pairs.append((i, (a ^ dy) * 8 + (b ^ dx) * 2 + (1 - c if flip else c)))
        return lax.ppermute(array, "seq", pairs)

    def other(array):
        return along_seq(array, flip=True)

    def in_hbm(array):
        return pltpu.with_memory_space_constraint(array, pltpu.HBM)

    b0 = other(grad_out)
    tie0 = jnp.zeros((8, DH), jnp.float32)
    key_own, _ = call(
        functools.partial(open_kernel, heads), (f32(heads * DH + 8, DH), f32(8, DH)),
        in_hbm(keys), in_hbm(values), in_hbm(log_decay), tie0,
        specs=[ANY] * 3 + [VMEM],
        scratch=[pltpu.VMEM((rows, width), jnp.bfloat16)] * 2 + [pltpu.VMEM((heads, rows), jnp.float32), pltpu.SemaphoreType.DMA((3,))],
    )
    a1 = along_z(grad_out)
    b1 = along_z(b0)

    key_other = other(key_own)
    sent, chip, b1 = call(
        functools.partial(chip_key_kernel, heads), (bf16(pair * DH + 16, DH), f32(pair * DH, DH), bf16(*grad_out.shape)),
        key_own, key_other, b1, specs=[VMEM] * 3,
    )
    from_x = [along_seq(sent, dx=d) for d in (2, 1, 3)]
    from_x = [from_x[1], from_x[0], from_x[2]]
    a2 = along_z(a1)
    b2 = along_z(b1)
    b2_here = other(b2)
    b1_here = other(call(gate_kernel, (bf16(*grad_out.shape),), b1, b2)[0])
    key_in, key_row, table, tail, b2 = call(
        functools.partial(row_key_kernel, pair),
        (f32(pair * DH, DH), f32(pair * DH, DH), f32(16 * pair, DH), bf16(16, DH), bf16(*grad_out.shape)),
        sent, chip, *from_x, b2, specs=[VMEM] * 6,
    )
    a3 = along_z(a2)
    b3 = along_z(b2)
    a4 = along_z(a3)

    qd = grad_out.shape[1]
    acc, w, qw, row, col = call(
        first_kernel,
        (f32(rows, width), bf16(2, width, qd), bf16(heads, 2 * DH, rows), f32(heads, rows), f32(rows, heads)),
        in_hbm(out_weight), in_hbm(grad_out), in_hbm(queries), in_hbm(log_decay), a1, b1_here, a2, b2_here, a3,
        specs=[ANY] * 4 + [VMEM] * 5,
        scratch=[
            pltpu.VMEM((6, width, qd), jnp.bfloat16), pltpu.VMEM((rows, qd), jnp.bfloat16),
            pltpu.VMEM((rows, width), jnp.bfloat16), pltpu.VMEM((heads, rows), jnp.float32), pltpu.SemaphoreType.DMA((11,)),
        ],
    )
    b3_here = other(call(gate_kernel, (bf16(*grad_out.shape),), b3, acc)[0])
    ga, grad_own = call(
        functools.partial(late_kernel, heads), (bf16(rows, width), f32(heads * DH, DH)), acc, a4, b3_here, w, qw
    )

    grad_other = other(grad_own)
    sent, chip = call(
        functools.partial(chip_grad_kernel, heads), (bf16(pair * DH, DH), f32(pair * DH, DH)),
        key_own, key_other, grad_own, grad_other, specs=[VMEM] * 4,
    )
    from_x = [along_seq(sent, dx=d) for d in (2, 1, 3)]
    from_x = [from_x[1], from_x[0], from_x[2]]
    def local_part(first):
        *parts, tie = call(
            functools.partial(local_kernel, pair, first), (f32(rows, pair * DH),) * 5 + (f32(8, DH),),
            queries, keys, values, ga, row, col,
        )
        dq, dk, dv, start_w, end_w = parts
        return (start_w, end_w, dq, dk, dv), tie

    low, tie = local_part(0)
    high, tie_high = local_part(pair)
    grad_in, *sent = call(
        functools.partial(row_grad_kernel, pair),
        (f32(pair * DH, DH),) + (bf16(pair * DH + 16, DH),) * 3,
        chip, from_x[0], from_x[2], from_x[1], key_row, table, tail, tie, specs=[VMEM] * 8,
    )
    from_y = [along_seq(sent[d - 1], dy=d) for d in (2, 1, 3)]
    from_y = [from_y[1], from_y[0], from_y[2]]
    (enter,) = call(
        functools.partial(enter_kernel, pair), (f32(2 * pair * DH, DH),),
        key_in, grad_in, table, from_y[1], from_y[0], from_y[2], tie_high, specs=[VMEM] * 7,
    )
    enter_other = other(enter)

    (own,) = call(
        functools.partial(own_kernel, 0), (f32(3, pair, rows, DH),), enter, key_other, grad_other, ga, keys, values, *low
    )
    return pl.pallas_call(
        functools.partial(rest_kernel, pair),
        out_shape=(f32(rows, width),) * 3,
        in_specs=[VMEM] * 12,
        out_specs=(ANY,) * 3,
        scratch_shapes=[pltpu.VMEM((3, pair, rows, DH), jnp.float32), pltpu.SemaphoreType.DMA((3, 3 * pair))],
        compiler_params=pltpu.CompilerParams(vmem_limit_bytes=24 * 2**20),
    )(enter_other, key_other, grad_other, ga, keys, values, *high, own)


def solution(mesh):
    return jax.shard_map(
        local,
        mesh=mesh,
        in_specs=(
            P("seq", "head"),
            P("seq", "head"),
            P("seq", "head"),
            P("head", "seq"),
            P("head", None),
            P("seq", "head"),
        ),
        out_specs=(P("seq", "head"), P("seq", "head"), P("seq", "head")),
        check_vma=False,
    )
```

```python
import functools

import jax
import jax.numpy as jnp
from jax import lax
from jax.experimental import pallas as pl
from jax.experimental.pallas import tpu as pltpu
from jax.sharding import PartitionSpec as P

DH = 128
NT = (((1,), (1,)), ((), ()))
NN = (((1,), (0,)), ((), ()))
TN = (((0,), (0,)), ((), ()))
VMEM = pl.BlockSpec(memory_space=pltpu.VMEM)
ANY = pl.BlockSpec(memory_space=pl.ANY)


def dot(a, b, dims):
    return lax.dot_general(a, b, dims, preferred_element_type=jnp.float32)


def pieces(x, n):
    out = []
    for _ in range(n):
        p = x.astype(jnp.bfloat16)
        out.append(p)
        x = x - p.astype(jnp.float32)
    return out


def call(kernel, outs, *args, specs=None, limit=24, scratch=(), aliases=None):
    return pl.pallas_call(
        kernel,
        out_shape=outs,
        in_specs=specs or [VMEM] * len(args),
        out_specs=tuple(VMEM for _ in outs),
        scratch_shapes=scratch,
        input_output_aliases=aliases or {},
        compiler_params=pltpu.CompilerParams(vmem_limit_bytes=limit * 2**20),
    )(*args)


def f32(*shape):
    return jax.ShapeDtypeStruct(shape, jnp.float32)


def bf16(*shape):
    return jax.ShapeDtypeStruct(shape, jnp.bfloat16)


def running(ld):
    n = ld.shape[1]
    s = lax.broadcasted_iota(jnp.int32, (n, n), 0)
    t = lax.broadcasted_iota(jnp.int32, (n, n), 1)
    upto = jnp.where(s <= t, 1.0, 0.0).astype(jnp.bfloat16)
    parts = pieces(ld, 3)
    return sum(dot(p, upto, NN) for p in parts), sum(dot(p, jnp.ones((n, DH), jnp.bfloat16), NN) for p in parts)


def running_columns(ld):
    n = ld.shape[1]
    s = lax.broadcasted_iota(jnp.int32, (n, n), 0)
    t = lax.broadcasted_iota(jnp.int32, (n, n), 1)
    since = jnp.where(s >= t, 1.0, 0.0).astype(jnp.bfloat16)
    return sum(dot(since, p, NT) for p in pieces(ld, 3))


def open_kernel(heads, k_hbm, v_hbm, ld_hbm, tie_ref, state_ref, tied_ref, k_ref, v_ref, ld_ref, sems):
    copies = [pltpu.make_async_copy(src, dst, sems.at[i]) for i, (src, dst) in enumerate(((ld_hbm, ld_ref), (k_hbm, k_ref), (v_hbm, v_ref)))]
    for copy in copies:
        copy.start()
    tied_ref[...] = tie_ref[...]
    n = k_ref.shape[0]
    copies[0].wait()
    row, total = running(ld_ref[...])
    state_ref[pl.ds(heads * DH, heads), :] = total
    state_ref[pl.ds(heads * DH + heads, 8 - heads), :] = jnp.zeros((8 - heads, DH), jnp.float32)
    for copy in copies[1:]:
        copy.wait()
    for h in range(heads):
        cols = slice(h * DH, (h + 1) * DH)
        kt = k_ref[:, cols].T.astype(jnp.float32) * jnp.exp(row[h : h + 1, n - 1 : n] - row[h : h + 1, :])
        hi, lo = pieces(kt, 2)
        v = v_ref[:, cols]
        state_ref[pl.ds(h * DH, DH), :] = dot(hi, v, NN) + dot(lo, v, NN)


def head_columns(position):
    return pl.ds(pl.multiple_of(lax.rem(core_index() * 2 + position, 4) * DH, DH), DH)


def local_kernel(heads, first, _, q_ref, k_ref, v_ref, ga_ref, row_ref, col_ref, dq_ref, dk_ref, dv_ref, start_ref, end_ref, tie_ref):
    n = q_ref.shape[0]
    step = n // 2
    s = lax.broadcasted_iota(jnp.int32, (step, step), 0)
    t = lax.broadcasted_iota(jnp.int32, (step, step), 1)
    keep = s <= t
    for i in range(heads):
        h = first + i
        cols, to = head_columns(h), slice(i * DH, (i + 1) * DH)
        col = col_ref[:, h : h + 1]
        start_ref[:, to] = jnp.broadcast_to(jnp.exp(col) * (1.0 / DH), (n, DH))
        end_ref[:, to] = jnp.broadcast_to(jnp.exp(row_ref[h : h + 1, n - 1 : n] - col) * (1.0 / DH), (n, DH))
        for sb in range(2):
            srows = slice(sb * step, (sb + 1) * step)
            k, v = k_ref[srows, cols], v_ref[srows, cols]
            col = col_ref[srows, h : h + 1]
            dk = dv = None
            for tb in range(sb, 2):
                trows = slice(tb * step, (tb + 1) * step)
                q, ga = q_ref[trows, cols], ga_ref[trows, cols]
                gap = row_ref[h : h + 1, trows] - col
                if tb == sb:
                    gap = jnp.where(keep, gap, -jnp.inf)
                weight = jnp.exp(gap) * (1.0 / DH)
                scores = (dot(k, q, NT) * weight).astype(jnp.bfloat16)
                grads = (dot(v, ga, NT) * weight).astype(jnp.bfloat16)
                dv_part = dot(scores, ga, NN)
                dk_part = dot(grads, q, NN)
                dv = dv_part if dv is None else dv + dv_part
                dk = dk_part if dk is None else dk + dk_part
                dq = dot(grads, k, TN)
                if sb == 0:
                    dq_ref[trows, to] = dq
                else:
                    dq_ref[trows, to] += dq
            dk_ref[srows, to] = dk
            dv_ref[srows, to] = dv
    tie_ref[...] = jnp.zeros(tie_ref.shape, jnp.float32)


def first_kernel(
    w_hbm, c_hbm, q_hbm, ld_hbm, a1, b1, a2, b2, a3, _,
    acc_ref, w_ref, qw_ref, row_ref, col_ref, near_ref, c_ref, q_ref, ld_ref, sems,
):
    z, side = lax.axis_index("head"), 1 - 2 * core_index()
    rows, width = c_ref.shape
    heads = ld_ref.shape[0]
    targets = [near_ref.at[i] for i in range(6)] + [w_ref.at[i] for i in range(2)]
    decays = pltpu.make_async_copy(ld_hbm, ld_ref, sems.at[10])
    decays.start()
    copies = [pltpu.make_async_copy(c_hbm, c_ref, sems.at[8]), pltpu.make_async_copy(q_hbm, q_ref, sems.at[9])]
    for i, (offset, target) in enumerate(zip((0, -1, 1, -2, 2, -3, 4, 3), targets)):
        at = lax.rem(z + offset * side + 8, 8) * width
        copies.append(pltpu.make_async_copy(w_hbm.at[:, pl.ds(pl.multiple_of(at, 128), width)], target, sems.at[i]))
    for copy in copies:
        copy.start()
    decays.wait()
    row, _ = running(ld_ref[...])
    col = running_columns(ld_ref[...])
    swap = core_index() == 1
    row_ref[...] = jnp.where(swap, jnp.concatenate([row[heads // 2 :], row[: heads // 2]], axis=0), row)
    col_ref[...] = jnp.where(swap, jnp.concatenate([col[:, heads // 2 :], col[:, : heads // 2]], axis=1), col)
    copies[1].wait()
    for h in range(heads):
        qt = q_ref[:, h * DH : (h + 1) * DH].T.astype(jnp.float32) * jnp.exp(row[h : h + 1, :])
        hi, lo = pieces(qt, 2)
        qw_ref[h, :DH, :] = hi
        qw_ref[h, DH:, :] = lo
    copies[0].wait()
    for copy in copies[2:]:
        copy.wait()
    half = rows // 2
    for part in range(2):
        at = pl.ds(part * half, half)
        acc = dot(c_ref[at, :], near_ref[0], NT)
        for i, ref in enumerate((a1, b1, a2, b2, a3)):
            acc += dot(ref[at, :], near_ref[i + 1], NT)
        acc_ref[at, :] = acc


def second_kernel(acc_ref, a4, w_ref, out_ref):
    half = acc_ref.shape[0] // 2
    for part in range(2):
        at = pl.ds(part * half, half)
        out_ref[at, :] = acc_ref[at, :] + dot(a4[at, :], w_ref[0], NT)


def late_kernel(heads, acc_ref, a4, b3, w_ref, qw_ref, ga_ref, own_ref, theirs_ref):
    half = acc_ref.shape[0] // 2
    for part in range(2):
        at = pl.ds(part * half, half)
        ga_ref[at, :] = (
            acc_ref[at, :] + dot(a4[at, :], w_ref[0], NT) + dot(b3[at, :], w_ref[1], NT)
        ).astype(jnp.bfloat16)
    for position in range(heads):
        h = lax.rem(core_index() * (heads // 2) + position, heads)
        both = dot(qw_ref[h], ga_ref[:, head_columns(position)], NN)
        to = own_ref if position < heads // 2 else theirs_ref
        to[pl.ds(position % (heads // 2) * DH, DH), :] = both[:DH] + both[DH:]


def gate_kernel(x_ref, *refs):
    refs[-1][...] = x_ref[...]


def core_index():
    return lax.rem(lax.axis_index("seq"), 2)


def x_index():
    return lax.rem(lax.div(lax.axis_index("seq"), 2), 4)


def y_index():
    return lax.div(lax.axis_index("seq"), 8)


def one_row(tile, i):
    return jnp.sum(jnp.where(lax.broadcasted_iota(jnp.int32, tile.shape, 0) == i, tile, 0.0), axis=0, keepdims=True)


def tail_of(totals):
    parts = [[p.astype(jnp.float32) for p in pieces(t, 3)] for t in totals]
    at = lax.broadcasted_iota(jnp.int32, (16, DH), 0)
    out = jnp.zeros((16, DH), jnp.float32)
    for j, three in enumerate(parts):
        for i, part in enumerate(three):
            out = jnp.where(at == 3 * j + i, part, out)
    return out.astype(jnp.bfloat16)


def total_in(tail, j):
    tail = tail.astype(jnp.float32)
    return one_row(tail, 3 * j) + one_row(tail, 3 * j + 1) + one_row(tail, 3 * j + 2)


def chip_key_kernel(heads, key_ref, key_other, tie_ref, sent_ref, chip_ref, tied_ref):
    tied_ref[...] = tie_ref[...]
    core = core_index()
    pair = heads // 2
    first = core == 0
    totals = []
    for j in range(pair):
        h = core * pair + j
        mine = one_row(key_ref[heads * DH :, :], h)
        others = one_row(key_other[heads * DH :, :], h)
        totals.append(mine + others)
        at = pl.ds(pl.multiple_of(h * DH, DH), DH)
        key = jnp.where(first, jnp.exp(others), 1.0) * key_ref[at, :] + jnp.where(first, 1.0, jnp.exp(mine)) * key_other[at, :]
        chip_ref[pl.ds(j * DH, DH), :] = key
        sent_ref[pl.ds(j * DH, DH), :] = key.astype(jnp.bfloat16)
    sent_ref[pl.ds(pair * DH, 16), :] = tail_of(totals)


def chip_grad_kernel(heads, key_ref, key_other, grad_ref, grad_other, sent_ref, chip_ref):
    core = core_index()
    pair = heads // 2
    first = core == 0
    for j in range(pair):
        h = core * pair + j
        mine = jnp.exp(one_row(key_ref[heads * DH :, :], h))
        others = jnp.exp(one_row(key_other[heads * DH :, :], h))
        at = pl.ds(j * DH, DH)
        grad = jnp.where(first, 1.0, others) * grad_ref[at, :] + jnp.where(first, mine, 1.0) * grad_other[at, :]
        chip_ref[pl.ds(j * DH, DH), :] = grad
        sent_ref[pl.ds(j * DH, DH), :] = grad.astype(jnp.bfloat16)


def flag(condition):
    return jnp.where(condition, 1.0, 0.0)


def places(x):
    return [jnp.bitwise_xor(x, d) for d in range(4)]


def between(totals, place, low, high):
    return sum(t * flag((low < p) & (p < high)) for t, p in zip(totals, place))


def row_key_kernel(pair, sent_ref, chip_ref, r1, r3, r2, in_ref, whole_ref, table_ref, tail_ref):
    x = x_index()
    n = pair * DH
    refs = (sent_ref, r1, r2, r3)
    place = places(x)
    tails = [ref[pl.ds(n, 16), :] for ref in refs]
    row_totals = []
    for j in range(pair):
        totals = [total_in(tail, j) for tail in tails]
        at = pl.ds(j * DH, DH)
        inside = 0.0
        whole = jnp.exp(between(totals, place, x, 4)) * chip_ref[at, :]
        for d in range(1, 4):
            state = refs[d][at, :].astype(jnp.float32)
            whole += jnp.exp(between(totals, place, place[d], 4)) * state
            inside += jnp.exp(between(totals, place, place[d], x)) * flag(place[d] < x) * state
        in_ref[at, :] = inside
        whole_ref[at, :] = whole
        lines = [jnp.exp(between(totals, place, -1, p)) for p in place]
        lines += [jnp.exp(between(totals, place, x, p)) * flag(p > x) for p in place[1:]]
        lines += [jnp.exp(between(totals, place, -1, x)), jnp.exp(between(totals, place, x, 4))]
        for i, line in enumerate(lines):
            table_ref[pl.ds(16 * j + i, 1), :] = line
        table_ref[pl.ds(16 * j + 9, 7), :] = jnp.zeros((7, DH), jnp.float32)
        row_totals.append(sum(totals))
    tail_ref[...] = tail_of(row_totals)


def row_grad_kernel(pair, chip_ref, r1, r3, r2, whole_key, table_ref, tail_ref, _, in_ref, s1, s2, s3):
    y = y_index()
    n = pair * DH
    refs = (r1, r2, r3)

    def line(j, i):
        return table_ref[pl.ds(16 * j + i, 1), :]

    for j in range(pair):
        at = pl.ds(j * DH, DH)
        inside = 0.0
        whole = line(j, 0) * chip_ref[at, :]
        for d in range(3):
            state = refs[d][at, :].astype(jnp.float32)
            whole += line(j, 1 + d) * state
            inside += line(j, 4 + d) * state
        in_ref[at, :] = inside
        for dy, ref in ((1, s1), (2, s2), (3, s3)):
            ref[at, :] = jnp.where(jnp.bitwise_xor(y, dy) > y, whole_key[at, :], whole).astype(jnp.bfloat16)
    for ref in (s1, s2, s3):
        ref[pl.ds(n, 16), :] = tail_ref[...]


def enter_kernel(pair, key_in, grad_in, table_ref, r2, r1, r3, _, enter_ref):
    y = y_index()
    n = pair * DH
    refs = (r1, r2, r3)
    place = places(y)[1:]
    tails = [ref[pl.ds(n, 16), :] for ref in refs]
    for j in range(pair):
        totals = [total_in(tail, j) for tail in tails]
        at = pl.ds(j * DH, DH)
        key, grad = key_in[at, :], grad_in[at, :]
        into, out = table_ref[pl.ds(16 * j + 7, 1), :], table_ref[pl.ds(16 * j + 8, 1), :]
        for d in range(3):
            p = place[d]
            gap = sum(t * flag(((p < q) & (q < y)) | ((y < q) & (q < p))) for t, q in zip(totals, place))
            weight = jnp.exp(gap)
            state = refs[d][at, :].astype(jnp.float32)
            key += into * weight * flag(p < y) * state
            grad += out * weight * flag(p > y) * state
        enter_ref[at, :] = key
        enter_ref[pl.ds((pair + j) * DH, DH), :] = grad


def closed(first, i, part, enter_ref, key_other, grad_other, ga_ref, k_ref, v_ref, start_w, end_w, dq, dk, dv, states):
    core = core_index()
    heads = key_other.shape[0] // DH
    pair = heads // 2
    cols = head_columns(first + i)
    if i not in states:
        h = lax.rem(core * pair + first + i, heads)
        key = enter_ref[pl.ds(i * DH, DH), :]
        grad = enter_ref[pl.ds((pair + i) * DH, DH), :]
        decay = jnp.exp(one_row(key_other[heads * DH :, :], h))
        si = jnp.where(core == 0, key, decay * key + key_other[cols, :])
        so = jnp.where(core == 0, decay * grad + grad_other[pl.ds(i * DH, DH), :], grad)
        hi, lo = pieces(so, 2)
        states[i] = jnp.concatenate(pieces(si, 2), axis=0), jnp.concatenate([hi, lo], axis=0), jnp.concatenate([hi, lo], axis=1)
    si, so, so_wide = states[i]
    mine = slice(i * DH, (i + 1) * DH)
    step = ga_ref.shape[0] // 4
    rows = pl.ds(part * step, step)

    def fold(x):
        return x[:, :DH] + x[:, DH:]

    return (
        dq[rows, mine] + start_w[rows, mine] * fold(dot(ga_ref[rows, cols], si, NT)),
        dk[rows, mine] + end_w[rows, mine] * fold(dot(v_ref[rows, cols], so, NT)),
        dv[rows, mine] + end_w[rows, mine] * fold(dot(k_ref[rows, cols], so_wide, NN)),
    )


def own_kernel(first, *refs):
    *inputs, out_ref = refs
    step = out_ref.shape[2] // 4
    states = {}
    for i in range(out_ref.shape[1]):
        for part in range(4):
            for j, value in enumerate(closed(first, i, part, *inputs, states)):
                out_ref[j, i, pl.ds(part * step, step)] = value


def rest_kernel(first, *refs):
    *inputs, own_ref, gq_ref, gk_ref, gv_ref, room, sems = refs
    outs = (gq_ref, gk_ref, gv_ref)
    pair, n = own_ref.shape[1:3]
    step = n // 4
    copies = []

    def send(src, j, position, at, sem):
        copy = pltpu.make_async_copy(src, outs[j].at[at, head_columns(position)], sem)
        copy.start()
        copies.append(copy)

    for i in range(pair):
        for j in range(3):
            send(own_ref.at[j, i], j, i, pl.ds(0, n), sems.at[j, i])
    states = {}
    for i in range(pair):
        for part in range(4):
            for j, value in enumerate(closed(first, i, part, *inputs, states)):
                room[j, i, pl.ds(part * step, step)] = value
            if part % 2:
                at = pl.ds((part - 1) * step, 2 * step)
                for j in range(3):
                    send(room.at[j, i, at], j, first + i, at, sems.at[j, pair + 2 * i + part // 2])
    for copy in copies:
        copy.wait()


def local(queries, keys, values, log_decay, out_weight, grad_out):
    rows, width = queries.shape
    heads = log_decay.shape[0]
    pair = heads // 2

    def along_z(array):
        pairs = []
        for i in range(32):
            for j in range(8):
                pairs.append((i * 8 + j, i * 8 + (j + (1 if i % 2 == 0 else -1)) % 8))
        return lax.ppermute(array, ("seq", "head"), pairs)

    def along_seq(array, dy=0, dx=0, flip=False):
        pairs = []
        for i in range(32):
            a, b, c = i // 8, (i // 2) % 4, i % 2
            pairs.append((i, (a ^ dy) * 8 + (b ^ dx) * 2 + (1 - c if flip else c)))
        return lax.ppermute(array, "seq", pairs)

    def other(array):
        return along_seq(array, flip=True)

    def in_hbm(array):
        return pltpu.with_memory_space_constraint(array, pltpu.HBM)

    b0 = other(grad_out)
    tie0 = jnp.zeros((8, DH), jnp.float32)
    key_own, _ = call(
        functools.partial(open_kernel, heads), (f32(heads * DH + 8, DH), f32(8, DH)),
        in_hbm(keys), in_hbm(values), in_hbm(log_decay), tie0,
        specs=[ANY] * 3 + [VMEM],
        scratch=[pltpu.VMEM((rows, width), jnp.bfloat16)] * 2 + [pltpu.VMEM((heads, rows), jnp.float32), pltpu.SemaphoreType.DMA((3,))],
    )
    a1 = along_z(grad_out)
    b1 = along_z(b0)

    key_other = other(key_own)
    sent, chip, b1 = call(
        functools.partial(chip_key_kernel, heads), (bf16(pair * DH + 16, DH), f32(pair * DH, DH), bf16(*grad_out.shape)),
        key_own, key_other, b1, specs=[VMEM] * 3,
    )
    from_x = [along_seq(sent, dx=d) for d in (2, 1, 3)]
    from_x = [from_x[1], from_x[0], from_x[2]]
    a2 = along_z(a1)
    b2 = along_z(b1)
    b2_here = other(b2)
    b1_here = other(call(gate_kernel, (bf16(*grad_out.shape),), b1, b2)[0])
    key_in, key_row, table, tail = call(
        functools.partial(row_key_kernel, pair),
        (f32(pair * DH, DH), f32(pair * DH, DH), f32(16 * pair, DH), bf16(16, DH)),
        sent, chip, from_x[0], from_x[2], from_x[1], specs=[VMEM] * 5,
    )
    a3 = along_z(a2)
    b3 = along_z(call(gate_kernel, (bf16(*grad_out.shape),), b2, from_x[0], from_x[2], from_x[1])[0])
    a4 = along_z(a3)

    qd = grad_out.shape[1]
    acc, w, qw, row, col = call(
        first_kernel,
        (f32(rows, width), bf16(2, width, qd), bf16(heads, 2 * DH, rows), f32(heads, rows), f32(rows, heads)),
        in_hbm(out_weight), in_hbm(grad_out), in_hbm(queries), in_hbm(log_decay), a1, b1_here, a2, b2_here, a3, tail,
        specs=[ANY] * 4 + [VMEM] * 6,
        scratch=[
            pltpu.VMEM((6, width, qd), jnp.bfloat16), pltpu.VMEM((rows, qd), jnp.bfloat16),
            pltpu.VMEM((rows, width), jnp.bfloat16), pltpu.VMEM((heads, rows), jnp.float32), pltpu.SemaphoreType.DMA((11,)),
        ],
    )
    b3_here = other(call(gate_kernel, (bf16(*grad_out.shape),), b3, acc)[0])
    ga, grad_own, grad_theirs = call(
        functools.partial(late_kernel, heads), (bf16(rows, width), f32(pair * DH, DH), f32(pair * DH, DH)), acc, a4, b3_here, w, qw
    )

    grad_other = other(grad_theirs)
    grad_rest = other(grad_own)
    sent, chip = call(
        functools.partial(chip_grad_kernel, heads), (bf16(pair * DH, DH), f32(pair * DH, DH)),
        key_own, key_other, grad_own, grad_other, specs=[VMEM] * 4,
    )
    from_x = [along_seq(sent, dx=d) for d in (2, 1, 3)]
    from_x = [from_x[1], from_x[0], from_x[2]]
    def local_part(first, after):
        *parts, tie = call(
            functools.partial(local_kernel, pair, first), (f32(rows, pair * DH),) * 5 + (f32(8, DH),),
            after, queries, keys, values, ga, row, col,
        )
        dq, dk, dv, start_w, end_w = parts
        return (start_w, end_w, dq, dk, dv), tie

    low, tie = local_part(0, row)
    high, tie_high = local_part(pair, grad_rest)
    grad_in, *sent = call(
        functools.partial(row_grad_kernel, pair),
        (f32(pair * DH, DH),) + (bf16(pair * DH + 16, DH),) * 3,
        chip, from_x[0], from_x[2], from_x[1], key_row, table, tail, tie, specs=[VMEM] * 8,
    )
    from_y = [along_seq(sent[d - 1], dy=d) for d in (2, 1, 3)]
    from_y = [from_y[1], from_y[0], from_y[2]]
    (enter,) = call(
        functools.partial(enter_kernel, pair), (f32(2 * pair * DH, DH),),
        key_in, grad_in, table, from_y[1], from_y[0], from_y[2], tie_high, specs=[VMEM] * 7,
    )
    enter_other = other(enter)

    (own,) = call(
        functools.partial(own_kernel, 0), (f32(3, pair, rows, DH),), enter, key_other, grad_other, ga, keys, values, *low
    )
    return pl.pallas_call(
        functools.partial(rest_kernel, pair),
        out_shape=(f32(rows, width),) * 3,
        in_specs=[VMEM] * 12,
        out_specs=(ANY,) * 3,
        scratch_shapes=[pltpu.VMEM((3, pair, rows, DH), jnp.float32), pltpu.SemaphoreType.DMA((3, 3 * pair))],
        compiler_params=pltpu.CompilerParams(vmem_limit_bytes=24 * 2**20),
    )(enter_other, key_other, grad_rest, ga, keys, values, *high, own)


def solution(mesh):
    return jax.shard_map(
        local,
        mesh=mesh,
        in_specs=(
            P("seq", "head"),
            P("seq", "head"),
            P("seq", "head"),
            P("head", "seq"),
            P("head", None),
            P("seq", "head"),
        ),
        out_specs=(P("seq", "head"), P("seq", "head"), P("seq", "head")),
        check_vma=False,
    )
```

```python
import functools

import jax
import jax.numpy as jnp
from jax import lax
from jax.experimental import pallas as pl
from jax.experimental.pallas import tpu as pltpu
from jax.sharding import PartitionSpec as P

DH = 128
NT = (((1,), (1,)), ((), ()))
NN = (((1,), (0,)), ((), ()))
TN = (((0,), (0,)), ((), ()))
VMEM = pl.BlockSpec(memory_space=pltpu.VMEM)
ANY = pl.BlockSpec(memory_space=pl.ANY)


def dot(a, b, dims):
    return lax.dot_general(a, b, dims, preferred_element_type=jnp.float32)


def pieces(x, n):
    out = []
    for _ in range(n):
        p = x.astype(jnp.bfloat16)
        out.append(p)
        x = x - p.astype(jnp.float32)
    return out


def call(kernel, outs, *args, specs=None, limit=24, scratch=(), aliases=None):
    return pl.pallas_call(
        kernel,
        out_shape=outs,
        in_specs=specs or [VMEM] * len(args),
        out_specs=tuple(VMEM for _ in outs),
        scratch_shapes=scratch,
        input_output_aliases=aliases or {},
        compiler_params=pltpu.CompilerParams(vmem_limit_bytes=limit * 2**20),
    )(*args)


def f32(*shape):
    return jax.ShapeDtypeStruct(shape, jnp.float32)


def bf16(*shape):
    return jax.ShapeDtypeStruct(shape, jnp.bfloat16)


def running(ld):
    n = ld.shape[1]
    s = lax.broadcasted_iota(jnp.int32, (n, n), 0)
    t = lax.broadcasted_iota(jnp.int32, (n, n), 1)
    upto = jnp.where(s <= t, 1.0, 0.0).astype(jnp.bfloat16)
    parts = pieces(ld, 3)
    return sum(dot(p, upto, NN) for p in parts), sum(dot(p, jnp.ones((n, DH), jnp.bfloat16), NN) for p in parts)


def running_columns(ld):
    n = ld.shape[1]
    s = lax.broadcasted_iota(jnp.int32, (n, n), 0)
    t = lax.broadcasted_iota(jnp.int32, (n, n), 1)
    since = jnp.where(s >= t, 1.0, 0.0).astype(jnp.bfloat16)
    return sum(dot(since, p, NT) for p in pieces(ld, 3))


def open_kernel(heads, k_hbm, v_hbm, ld_hbm, tie_ref, state_ref, tied_ref, k_ref, v_ref, ld_ref, sems):
    copies = [pltpu.make_async_copy(src, dst, sems.at[i]) for i, (src, dst) in enumerate(((ld_hbm, ld_ref), (k_hbm, k_ref), (v_hbm, v_ref)))]
    for copy in copies:
        copy.start()
    tied_ref[...] = tie_ref[...]
    n = k_ref.shape[0]
    copies[0].wait()
    row, total = running(ld_ref[...])
    state_ref[pl.ds(heads * DH, heads), :] = total
    state_ref[pl.ds(heads * DH + heads, 8 - heads), :] = jnp.zeros((8 - heads, DH), jnp.float32)
    for copy in copies[1:]:
        copy.wait()
    for h in range(heads):
        cols = slice(h * DH, (h + 1) * DH)
        kt = k_ref[:, cols].T.astype(jnp.float32) * jnp.exp(row[h : h + 1, n - 1 : n] - row[h : h + 1, :])
        hi, lo = pieces(kt, 2)
        v = v_ref[:, cols]
        state_ref[pl.ds(h * DH, DH), :] = dot(hi, v, NN) + dot(lo, v, NN)


def head_columns(position):
    return pl.ds(pl.multiple_of(lax.rem(core_index() * 2 + position, 4) * DH, DH), DH)


def local_kernel(heads, first, _, q_ref, k_ref, v_ref, ga_ref, row_ref, col_ref, dq_ref, dk_ref, dv_ref, start_ref, end_ref, tie_ref):
    n = q_ref.shape[0]
    step = n // 2
    s = lax.broadcasted_iota(jnp.int32, (step, step), 0)
    t = lax.broadcasted_iota(jnp.int32, (step, step), 1)
    keep = s <= t
    for i in range(heads):
        h = first + i
        cols, to = head_columns(h), slice(i * DH, (i + 1) * DH)
        col = col_ref[:, h : h + 1]
        start_ref[:, to] = jnp.broadcast_to(jnp.exp(col) * (1.0 / DH), (n, DH))
        end_ref[:, to] = jnp.broadcast_to(jnp.exp(row_ref[h : h + 1, n - 1 : n] - col) * (1.0 / DH), (n, DH))
        for sb in range(2):
            srows = slice(sb * step, (sb + 1) * step)
            k, v = k_ref[srows, cols], v_ref[srows, cols]
            col = col_ref[srows, h : h + 1]
            dk = dv = None
            for tb in range(sb, 2):
                trows = slice(tb * step, (tb + 1) * step)
                q, ga = q_ref[trows, cols], ga_ref[trows, cols]
                gap = row_ref[h : h + 1, trows] - col
                if tb == sb:
                    gap = jnp.where(keep, gap, -jnp.inf)
                weight = jnp.exp(gap) * (1.0 / DH)
                scores = (dot(k, q, NT) * weight).astype(jnp.bfloat16)
                grads = (dot(v, ga, NT) * weight).astype(jnp.bfloat16)
                dv_part = dot(scores, ga, NN)
                dk_part = dot(grads, q, NN)
                dv = dv_part if dv is None else dv + dv_part
                dk = dk_part if dk is None else dk + dk_part
                dq = dot(grads, k, TN)
                if sb == 0:
                    dq_ref[trows, to] = dq
                else:
                    dq_ref[trows, to] += dq
            dk_ref[srows, to] = dk
            dv_ref[srows, to] = dv
    tie_ref[...] = jnp.zeros(tie_ref.shape, jnp.float32)


def first_kernel(
    w_hbm, c_hbm, q_hbm, ld_hbm, a1, b1, a2, b2, a3, _,
    acc_ref, w_ref, qw_ref, row_ref, col_ref, near_ref, c_ref, q_ref, ld_ref, sems,
):
    z, side = lax.axis_index("head"), 1 - 2 * core_index()
    rows, width = c_ref.shape
    heads = ld_ref.shape[0]
    targets = [near_ref.at[i] for i in range(6)] + [w_ref.at[i] for i in range(2)]
    decays = pltpu.make_async_copy(ld_hbm, ld_ref, sems.at[10])
    decays.start()
    copies = [pltpu.make_async_copy(c_hbm, c_ref, sems.at[8]), pltpu.make_async_copy(q_hbm, q_ref, sems.at[9])]
    for i, (offset, target) in enumerate(zip((0, -1, 1, -2, 2, -3, 4, 3), targets)):
        at = lax.rem(z + offset * side + 8, 8) * width
        copies.append(pltpu.make_async_copy(w_hbm.at[:, pl.ds(pl.multiple_of(at, 128), width)], target, sems.at[i]))
    for copy in copies:
        copy.start()
    decays.wait()
    row, _ = running(ld_ref[...])
    col = running_columns(ld_ref[...])
    swap = core_index() == 1
    row_ref[...] = jnp.where(swap, jnp.concatenate([row[heads // 2 :], row[: heads // 2]], axis=0), row)
    col_ref[...] = jnp.where(swap, jnp.concatenate([col[:, heads // 2 :], col[:, : heads // 2]], axis=1), col)
    copies[1].wait()
    for h in range(heads):
        qt = q_ref[:, h * DH : (h + 1) * DH].T.astype(jnp.float32) * jnp.exp(row[h : h + 1, :])
        hi, lo = pieces(qt, 2)
        qw_ref[h, :DH, :] = hi
        qw_ref[h, DH:, :] = lo
    copies[0].wait()
    for copy in copies[2:]:
        copy.wait()
    half = rows // 2
    for part in range(2):
        at = pl.ds(part * half, half)
        acc = dot(c_ref[at, :], near_ref[0], NT)
        for i, ref in enumerate((a1, b1, a2, b2, a3)):
            acc += dot(ref[at, :], near_ref[i + 1], NT)
        acc_ref[at, :] = acc


def second_kernel(acc_ref, a4, w_ref, out_ref):
    half = acc_ref.shape[0] // 2
    for part in range(2):
        at = pl.ds(part * half, half)
        out_ref[at, :] = acc_ref[at, :] + dot(a4[at, :], w_ref[0], NT)


def late_kernel(heads, acc_ref, a4, b3, w_ref, qw_ref, ga_ref, own_ref, theirs_ref):
    half = acc_ref.shape[0] // 2
    for part in range(2):
        at = pl.ds(part * half, half)
        ga_ref[at, :] = (
            acc_ref[at, :] + dot(a4[at, :], w_ref[0], NT) + dot(b3[at, :], w_ref[1], NT)
        ).astype(jnp.bfloat16)
    for position in range(heads):
        h = lax.rem(core_index() * (heads // 2) + position, heads)
        both = dot(qw_ref[h], ga_ref[:, head_columns(position)], NN)
        to = own_ref if position < heads // 2 else theirs_ref
        to[pl.ds(position % (heads // 2) * DH, DH), :] = both[:DH] + both[DH:]


def gate_kernel(x_ref, *refs):
    refs[-1][...] = x_ref[...]


def core_index():
    return lax.rem(lax.axis_index("seq"), 2)


def x_index():
    return lax.rem(lax.div(lax.axis_index("seq"), 2), 4)


def y_index():
    return lax.div(lax.axis_index("seq"), 8)


def one_row(tile, i):
    return jnp.sum(jnp.where(lax.broadcasted_iota(jnp.int32, tile.shape, 0) == i, tile, 0.0), axis=0, keepdims=True)


def tail_of(totals):
    parts = [[p.astype(jnp.float32) for p in pieces(t, 3)] for t in totals]
    at = lax.broadcasted_iota(jnp.int32, (16, DH), 0)
    out = jnp.zeros((16, DH), jnp.float32)
    for j, three in enumerate(parts):
        for i, part in enumerate(three):
            out = jnp.where(at == 3 * j + i, part, out)
    return out.astype(jnp.bfloat16)


def total_in(tail, j):
    tail = tail.astype(jnp.float32)
    return one_row(tail, 3 * j) + one_row(tail, 3 * j + 1) + one_row(tail, 3 * j + 2)


def chip_key_kernel(heads, key_ref, key_other, tie_ref, sent_ref, chip_ref, tied_ref):
    tied_ref[...] = tie_ref[...]
    core = core_index()
    pair = heads // 2
    first = core == 0
    totals = []
    for j in range(pair):
        h = core * pair + j
        mine = one_row(key_ref[heads * DH :, :], h)
        others = one_row(key_other[heads * DH :, :], h)
        totals.append(mine + others)
        at = pl.ds(pl.multiple_of(h * DH, DH), DH)
        key = jnp.where(first, jnp.exp(others), 1.0) * key_ref[at, :] + jnp.where(first, 1.0, jnp.exp(mine)) * key_other[at, :]
        chip_ref[pl.ds(j * DH, DH), :] = key
        sent_ref[pl.ds(j * DH, DH), :] = key.astype(jnp.bfloat16)
    sent_ref[pl.ds(pair * DH, 16), :] = tail_of(totals)


def chip_grad_kernel(heads, key_ref, key_other, grad_ref, grad_other, sent_ref, chip_ref):
    core = core_index()
    pair = heads // 2
    first = core == 0
    for j in range(pair):
        h = core * pair + j
        mine = jnp.exp(one_row(key_ref[heads * DH :, :], h))
        others = jnp.exp(one_row(key_other[heads * DH :, :], h))
        at = pl.ds(j * DH, DH)
        grad = jnp.where(first, 1.0, others) * grad_ref[at, :] + jnp.where(first, mine, 1.0) * grad_other[at, :]
        chip_ref[pl.ds(j * DH, DH), :] = grad
        sent_ref[pl.ds(j * DH, DH), :] = grad.astype(jnp.bfloat16)


def flag(condition):
    return jnp.where(condition, 1.0, 0.0)


def places(x):
    return [jnp.bitwise_xor(x, d) for d in range(4)]


def between(totals, place, low, high):
    return sum(t * flag((low < p) & (p < high)) for t, p in zip(totals, place))


def row_key_kernel(pair, sent_ref, chip_ref, r1, r3, r2, in_ref, whole_ref, table_ref, tail_ref):
    x = x_index()
    n = pair * DH
    refs = (sent_ref, r1, r2, r3)
    place = places(x)
    tails = [ref[pl.ds(n, 16), :] for ref in refs]
    row_totals = []
    for j in range(pair):
        totals = [total_in(tail, j) for tail in tails]
        at = pl.ds(j * DH, DH)
        inside = 0.0
        whole = jnp.exp(between(totals, place, x, 4)) * chip_ref[at, :]
        for d in range(1, 4):
            state = refs[d][at, :].astype(jnp.float32)
            whole += jnp.exp(between(totals, place, place[d], 4)) * state
            inside += jnp.exp(between(totals, place, place[d], x)) * flag(place[d] < x) * state
        in_ref[at, :] = inside
        whole_ref[at, :] = whole
        lines = [jnp.exp(between(totals, place, -1, p)) for p in place]
        lines += [jnp.exp(between(totals, place, x, p)) * flag(p > x) for p in place[1:]]
        lines += [jnp.exp(between(totals, place, -1, x)), jnp.exp(between(totals, place, x, 4))]
        for i, line in enumerate(lines):
            table_ref[pl.ds(16 * j + i, 1), :] = line
        table_ref[pl.ds(16 * j + 9, 7), :] = jnp.zeros((7, DH), jnp.float32)
        row_totals.append(sum(totals))
    tail_ref[...] = tail_of(row_totals)


def row_grad_kernel(pair, chip_ref, r1, r3, r2, whole_key, table_ref, tail_ref, _, in_ref, s1, s2, s3):
    y = y_index()
    n = pair * DH
    refs = (r1, r2, r3)

    def line(j, i):
        return table_ref[pl.ds(16 * j + i, 1), :]

    for j in range(pair):
        at = pl.ds(j * DH, DH)
        inside = 0.0
        whole = line(j, 0) * chip_ref[at, :]
        for d in range(3):
            state = refs[d][at, :].astype(jnp.float32)
            whole += line(j, 1 + d) * state
            inside += line(j, 4 + d) * state
        in_ref[at, :] = inside
        for dy, ref in ((1, s1), (2, s2), (3, s3)):
            ref[at, :] = jnp.where(jnp.bitwise_xor(y, dy) > y, whole_key[at, :], whole).astype(jnp.bfloat16)
    for ref in (s1, s2, s3):
        ref[pl.ds(n, 16), :] = tail_ref[...]


def enter_kernel(pair, key_in, grad_in, table_ref, r2, r1, r3, _, enter_ref):
    y = y_index()
    n = pair * DH
    refs = (r1, r2, r3)
    place = places(y)[1:]
    tails = [ref[pl.ds(n, 16), :] for ref in refs]
    for j in range(pair):
        totals = [total_in(tail, j) for tail in tails]
        at = pl.ds(j * DH, DH)
        key, grad = key_in[at, :], grad_in[at, :]
        into, out = table_ref[pl.ds(16 * j + 7, 1), :], table_ref[pl.ds(16 * j + 8, 1), :]
        for d in range(3):
            p = place[d]
            gap = sum(t * flag(((p < q) & (q < y)) | ((y < q) & (q < p))) for t, q in zip(totals, place))
            weight = jnp.exp(gap)
            state = refs[d][at, :].astype(jnp.float32)
            key += into * weight * flag(p < y) * state
            grad += out * weight * flag(p > y) * state
        enter_ref[at, :] = key
        enter_ref[pl.ds((pair + j) * DH, DH), :] = grad


def closed(first, i, part, enter_ref, key_other, grad_other, ga_ref, k_ref, v_ref, start_w, end_w, dq, dk, dv, states):
    core = core_index()
    heads = key_other.shape[0] // DH
    pair = heads // 2
    cols = head_columns(first + i)
    if i not in states:
        h = lax.rem(core * pair + first + i, heads)
        key = enter_ref[pl.ds(i * DH, DH), :]
        grad = enter_ref[pl.ds((pair + i) * DH, DH), :]
        decay = jnp.exp(one_row(key_other[heads * DH :, :], h))
        si = jnp.where(core == 0, key, decay * key + key_other[cols, :])
        so = jnp.where(core == 0, decay * grad + grad_other[pl.ds(i * DH, DH), :], grad)
        hi, lo = pieces(so, 2)
        states[i] = jnp.concatenate(pieces(si, 2), axis=0), jnp.concatenate([hi, lo], axis=0), jnp.concatenate([hi, lo], axis=1)
    si, so, so_wide = states[i]
    mine = slice(i * DH, (i + 1) * DH)
    step = ga_ref.shape[0] // 4
    rows = pl.ds(part * step, step)

    def fold(x):
        return x[:, :DH] + x[:, DH:]

    return (
        dq[rows, mine] + start_w[rows, mine] * fold(dot(ga_ref[rows, cols], si, NT)),
        dk[rows, mine] + end_w[rows, mine] * fold(dot(v_ref[rows, cols], so, NT)),
        dv[rows, mine] + end_w[rows, mine] * fold(dot(k_ref[rows, cols], so_wide, NN)),
    )


def own_kernel(first, *refs):
    *inputs, gq_ref, gk_ref, gv_ref, out_ref, room, sems = refs
    outs = (gq_ref, gk_ref, gv_ref)
    n = out_ref.shape[2]
    step = n // 4
    states = {}
    copies = []
    for i in range(1 + out_ref.shape[1]):
        for part in range(4):
            at = pl.ds(part * step, step)
            for j, value in enumerate(closed(first, i, part, *inputs, states)):
                if i:
                    out_ref[j, i - 1, at] = value
                else:
                    room[j, at] = value
        if i == 0:
            for j in range(3):
                copy = pltpu.make_async_copy(room.at[j], outs[j].at[:, head_columns(first)], sems.at[j])
                copy.start()
                copies.append(copy)
    for copy in copies:
        copy.wait()


def rest_kernel(first, *refs):
    inputs, own_ref, (gq_ref, gk_ref, gv_ref, room, sems) = refs[:11], refs[11], refs[-5:]
    outs = (gq_ref, gk_ref, gv_ref)
    n = own_ref.shape[2]
    pair = room.shape[1]
    step = n // 4
    copies = []

    def send(src, j, position, at, sem):
        copy = pltpu.make_async_copy(src, outs[j].at[at, head_columns(position)], sem)
        copy.start()
        copies.append(copy)

    for j in range(3):
        send(own_ref.at[j, 0], j, 1, pl.ds(0, n), sems.at[j, 0])
    states = {}
    for i in range(pair):
        for part in range(4):
            for j, value in enumerate(closed(first, i, part, *inputs, states)):
                room[j, i, pl.ds(part * step, step)] = value
            if part % 2:
                at = pl.ds((part - 1) * step, 2 * step)
                for j in range(3):
                    send(room.at[j, i, at], j, first + i, at, sems.at[j, pair + 2 * i + part // 2])
    for copy in copies:
        copy.wait()


def local(queries, keys, values, log_decay, out_weight, grad_out):
    rows, width = queries.shape
    heads = log_decay.shape[0]
    pair = heads // 2

    def along_z(array):
        pairs = []
        for i in range(32):
            for j in range(8):
                pairs.append((i * 8 + j, i * 8 + (j + (1 if i % 2 == 0 else -1)) % 8))
        return lax.ppermute(array, ("seq", "head"), pairs)

    def along_seq(array, dy=0, dx=0, flip=False):
        pairs = []
        for i in range(32):
            a, b, c = i // 8, (i // 2) % 4, i % 2
            pairs.append((i, (a ^ dy) * 8 + (b ^ dx) * 2 + (1 - c if flip else c)))
        return lax.ppermute(array, "seq", pairs)

    def other(array):
        return along_seq(array, flip=True)

    def in_hbm(array):
        return pltpu.with_memory_space_constraint(array, pltpu.HBM)

    b0 = other(grad_out)
    tie0 = jnp.zeros((8, DH), jnp.float32)
    key_own, _ = call(
        functools.partial(open_kernel, heads), (f32(heads * DH + 8, DH), f32(8, DH)),
        in_hbm(keys), in_hbm(values), in_hbm(log_decay), tie0,
        specs=[ANY] * 3 + [VMEM],
        scratch=[pltpu.VMEM((rows, width), jnp.bfloat16)] * 2 + [pltpu.VMEM((heads, rows), jnp.float32), pltpu.SemaphoreType.DMA((3,))],
    )
    a1 = along_z(grad_out)
    b1 = along_z(b0)

    key_other = other(key_own)
    sent, chip, b1 = call(
        functools.partial(chip_key_kernel, heads), (bf16(pair * DH + 16, DH), f32(pair * DH, DH), bf16(*grad_out.shape)),
        key_own, key_other, b1, specs=[VMEM] * 3,
    )
    from_x = [along_seq(sent, dx=d) for d in (2, 1, 3)]
    from_x = [from_x[1], from_x[0], from_x[2]]
    a2 = along_z(a1)
    b2 = along_z(b1)
    b2_here = other(b2)
    b1_here = other(call(gate_kernel, (bf16(*grad_out.shape),), b1, b2)[0])
    key_in, key_row, table, tail = call(
        functools.partial(row_key_kernel, pair),
        (f32(pair * DH, DH), f32(pair * DH, DH), f32(16 * pair, DH), bf16(16, DH)),
        sent, chip, from_x[0], from_x[2], from_x[1], specs=[VMEM] * 5,
    )
    a3 = along_z(a2)
    b3 = along_z(call(gate_kernel, (bf16(*grad_out.shape),), b2, from_x[0], from_x[2], from_x[1])[0])
    a4 = along_z(a3)

    qd = grad_out.shape[1]
    acc, w, qw, row, col = call(
        first_kernel,
        (f32(rows, width), bf16(2, width, qd), bf16(heads, 2 * DH, rows), f32(heads, rows), f32(rows, heads)),
        in_hbm(out_weight), in_hbm(grad_out), in_hbm(queries), in_hbm(log_decay), a1, b1_here, a2, b2_here, a3, tail,
        specs=[ANY] * 4 + [VMEM] * 6,
        scratch=[
            pltpu.VMEM((6, width, qd), jnp.bfloat16), pltpu.VMEM((rows, qd), jnp.bfloat16),
            pltpu.VMEM((rows, width), jnp.bfloat16), pltpu.VMEM((heads, rows), jnp.float32), pltpu.SemaphoreType.DMA((11,)),
        ],
    )
    b3_here = other(call(gate_kernel, (bf16(*grad_out.shape),), b3, acc)[0])
    ga, grad_own, grad_theirs = call(
        functools.partial(late_kernel, heads), (bf16(rows, width), f32(pair * DH, DH), f32(pair * DH, DH)), acc, a4, b3_here, w, qw
    )

    grad_other = other(grad_theirs)
    grad_rest = other(grad_own)
    sent, chip = call(
        functools.partial(chip_grad_kernel, heads), (bf16(pair * DH, DH), f32(pair * DH, DH)),
        key_own, key_other, grad_own, grad_other, specs=[VMEM] * 4,
    )
    from_x = [along_seq(sent, dx=d) for d in (2, 1, 3)]
    from_x = [from_x[1], from_x[0], from_x[2]]
    def local_part(first, after):
        *parts, tie = call(
            functools.partial(local_kernel, pair, first), (f32(rows, pair * DH),) * 5 + (f32(8, DH),),
            after, queries, keys, values, ga, row, col,
        )
        dq, dk, dv, start_w, end_w = parts
        return (start_w, end_w, dq, dk, dv), tie

    low, tie = local_part(0, row)
    high, tie_high = local_part(pair, grad_rest)
    grad_in, *sent = call(
        functools.partial(row_grad_kernel, pair),
        (f32(pair * DH, DH),) + (bf16(pair * DH + 16, DH),) * 3,
        chip, from_x[0], from_x[2], from_x[1], key_row, table, tail, tie, specs=[VMEM] * 8,
    )
    from_y = [along_seq(sent[d - 1], dy=d) for d in (2, 1, 3)]
    from_y = [from_y[1], from_y[0], from_y[2]]
    (enter,) = call(
        functools.partial(enter_kernel, pair), (f32(2 * pair * DH, DH),),
        key_in, grad_in, table, from_y[1], from_y[0], from_y[2], tie_high, specs=[VMEM] * 7,
    )
    enter_other = other(enter)

    *done, own = pl.pallas_call(
        functools.partial(own_kernel, 0),
        out_shape=(f32(rows, width),) * 3 + (f32(3, 1, rows, DH),),
        in_specs=[VMEM] * 11,
        out_specs=(ANY,) * 3 + (VMEM,),
        scratch_shapes=[pltpu.VMEM((3, rows, DH), jnp.float32), pltpu.SemaphoreType.DMA((3,))],
        compiler_params=pltpu.CompilerParams(vmem_limit_bytes=24 * 2**20),
    )(enter, key_other, grad_other, ga, keys, values, *low)
    return tuple(
        pl.pallas_call(
            functools.partial(rest_kernel, pair),
            out_shape=(f32(rows, width),) * 3,
            in_specs=[VMEM] * 12 + [ANY] * 3,
            out_specs=(ANY,) * 3,
            scratch_shapes=[pltpu.VMEM((3, pair, rows, DH), jnp.float32), pltpu.SemaphoreType.DMA((3, 3 * pair))],
            input_output_aliases={12 + j: j for j in range(3)},
            compiler_params=pltpu.CompilerParams(vmem_limit_bytes=24 * 2**20),
        )(enter_other, key_other, grad_rest, ga, keys, values, *high, own, *done)
    )


def solution(mesh):
    return jax.shard_map(
        local,
        mesh=mesh,
        in_specs=(
            P("seq", "head"),
            P("seq", "head"),
            P("seq", "head"),
            P("head", "seq"),
            P("head", None),
            P("seq", "head"),
        ),
        out_specs=(P("seq", "head"), P("seq", "head"), P("seq", "head")),
        check_vma=False,
    )
```

```python
import functools

import jax
import jax.numpy as jnp
from jax import lax
from jax.experimental import pallas as pl
from jax.experimental.pallas import tpu as pltpu
from jax.sharding import PartitionSpec as P

DH = 128
NT = (((1,), (1,)), ((), ()))
NN = (((1,), (0,)), ((), ()))
TN = (((0,), (0,)), ((), ()))
VMEM = pl.BlockSpec(memory_space=pltpu.VMEM)
ANY = pl.BlockSpec(memory_space=pl.ANY)


def dot(a, b, dims):
    return lax.dot_general(a, b, dims, preferred_element_type=jnp.float32)


def pieces(x, n):
    out = []
    for _ in range(n):
        p = x.astype(jnp.bfloat16)
        out.append(p)
        x = x - p.astype(jnp.float32)
    return out


def call(kernel, outs, *args, specs=None, limit=24, scratch=(), aliases=None):
    return pl.pallas_call(
        kernel,
        out_shape=outs,
        in_specs=specs or [VMEM] * len(args),
        out_specs=tuple(VMEM for _ in outs),
        scratch_shapes=scratch,
        input_output_aliases=aliases or {},
        compiler_params=pltpu.CompilerParams(vmem_limit_bytes=limit * 2**20),
    )(*args)


def f32(*shape):
    return jax.ShapeDtypeStruct(shape, jnp.float32)


def bf16(*shape):
    return jax.ShapeDtypeStruct(shape, jnp.bfloat16)


def running(ld):
    n = ld.shape[1]
    s = lax.broadcasted_iota(jnp.int32, (n, n), 0)
    t = lax.broadcasted_iota(jnp.int32, (n, n), 1)
    upto = jnp.where(s <= t, 1.0, 0.0).astype(jnp.bfloat16)
    parts = pieces(ld, 3)
    return sum(dot(p, upto, NN) for p in parts), sum(dot(p, jnp.ones((n, DH), jnp.bfloat16), NN) for p in parts)


def running_columns(ld):
    n = ld.shape[1]
    s = lax.broadcasted_iota(jnp.int32, (n, n), 0)
    t = lax.broadcasted_iota(jnp.int32, (n, n), 1)
    since = jnp.where(s >= t, 1.0, 0.0).astype(jnp.bfloat16)
    return sum(dot(since, p, NT) for p in pieces(ld, 3))


def open_kernel(heads, k_hbm, v_hbm, ld_hbm, tie_ref, state_ref, tied_ref, k_ref, v_ref, ld_ref, sems):
    copies = [pltpu.make_async_copy(src, dst, sems.at[i]) for i, (src, dst) in enumerate(((ld_hbm, ld_ref), (k_hbm, k_ref), (v_hbm, v_ref)))]
    for copy in copies:
        copy.start()
    tied_ref[...] = tie_ref[...]
    n = k_ref.shape[0]
    copies[0].wait()
    row, total = running(ld_ref[...])
    state_ref[pl.ds(heads * DH, heads), :] = total
    state_ref[pl.ds(heads * DH + heads, 8 - heads), :] = jnp.zeros((8 - heads, DH), jnp.float32)
    for copy in copies[1:]:
        copy.wait()
    for h in range(heads):
        cols = slice(h * DH, (h + 1) * DH)
        kt = k_ref[:, cols].T.astype(jnp.float32) * jnp.exp(row[h : h + 1, n - 1 : n] - row[h : h + 1, :])
        hi, lo = pieces(kt, 2)
        v = v_ref[:, cols]
        state_ref[pl.ds(h * DH, DH), :] = dot(hi, v, NN) + dot(lo, v, NN)


def head_columns(position):
    return pl.ds(pl.multiple_of(lax.rem(core_index() * 2 + position, 4) * DH, DH), DH)


def local_kernel(heads, first, _, q_ref, k_ref, v_ref, ga_ref, row_ref, col_ref, dq_ref, dk_ref, dv_ref, start_ref, end_ref, tie_ref):
    n = q_ref.shape[0]
    step = n // 2
    s = lax.broadcasted_iota(jnp.int32, (step, step), 0)
    t = lax.broadcasted_iota(jnp.int32, (step, step), 1)
    keep = s <= t
    for i in range(heads):
        h = first + i
        cols, to = head_columns(h), slice(i * DH, (i + 1) * DH)
        col = col_ref[:, h : h + 1]
        start_ref[:, to] = jnp.broadcast_to(jnp.exp(col) * (1.0 / DH), (n, DH))
        end_ref[:, to] = jnp.broadcast_to(jnp.exp(row_ref[h : h + 1, n - 1 : n] - col) * (1.0 / DH), (n, DH))
        for sb in range(2):
            srows = slice(sb * step, (sb + 1) * step)
            k, v = k_ref[srows, cols], v_ref[srows, cols]
            col = col_ref[srows, h : h + 1]
            dk = dv = None
            for tb in range(sb, 2):
                trows = slice(tb * step, (tb + 1) * step)
                q, ga = q_ref[trows, cols], ga_ref[trows, cols]
                gap = row_ref[h : h + 1, trows] - col
                if tb == sb:
                    gap = jnp.where(keep, gap, -jnp.inf)
                weight = jnp.exp(gap) * (1.0 / DH)
                scores = (dot(k, q, NT) * weight).astype(jnp.bfloat16)
                grads = (dot(v, ga, NT) * weight).astype(jnp.bfloat16)
                dv_part = dot(scores, ga, NN)
                dk_part = dot(grads, q, NN)
                dv = dv_part if dv is None else dv + dv_part
                dk = dk_part if dk is None else dk + dk_part
                dq = dot(grads, k, TN)
                if sb == 0:
                    dq_ref[trows, to] = dq
                else:
                    dq_ref[trows, to] += dq
            dk_ref[srows, to] = dk
            dv_ref[srows, to] = dv
    tie_ref[...] = jnp.zeros(tie_ref.shape, jnp.float32)


def first_kernel(
    w_hbm, c_hbm, q_hbm, ld_hbm, a1, b1, a2, b2, a3, _,
    acc_ref, w_ref, qw_ref, row_ref, col_ref, near_ref, c_ref, q_ref, ld_ref, sems,
):
    z, side = lax.axis_index("head"), 1 - 2 * core_index()
    rows, width = c_ref.shape
    heads = ld_ref.shape[0]
    targets = [near_ref.at[i] for i in range(6)] + [w_ref.at[i] for i in range(2)]
    decays = pltpu.make_async_copy(ld_hbm, ld_ref, sems.at[10])
    decays.start()
    copies = [pltpu.make_async_copy(c_hbm, c_ref, sems.at[8]), pltpu.make_async_copy(q_hbm, q_ref, sems.at[9])]
    for i, (offset, target) in enumerate(zip((0, -1, 1, -2, 2, -3, 4, 3), targets)):
        at = lax.rem(z + offset * side + 8, 8) * width
        copies.append(pltpu.make_async_copy(w_hbm.at[:, pl.ds(pl.multiple_of(at, 128), width)], target, sems.at[i]))
    for copy in copies:
        copy.start()
    decays.wait()
    row, _ = running(ld_ref[...])
    col = running_columns(ld_ref[...])
    swap = core_index() == 1
    row_ref[...] = jnp.where(swap, jnp.concatenate([row[heads // 2 :], row[: heads // 2]], axis=0), row)
    col_ref[...] = jnp.where(swap, jnp.concatenate([col[:, heads // 2 :], col[:, : heads // 2]], axis=1), col)
    copies[1].wait()
    for h in range(heads):
        qt = q_ref[:, h * DH : (h + 1) * DH].T.astype(jnp.float32) * jnp.exp(row[h : h + 1, :])
        hi, lo = pieces(qt, 2)
        qw_ref[h, :DH, :] = hi
        qw_ref[h, DH:, :] = lo
    copies[0].wait()
    for copy in copies[2:]:
        copy.wait()
    half = rows // 2
    for part in range(2):
        at = pl.ds(part * half, half)
        acc = dot(c_ref[at, :], near_ref[0], NT)
        for i, ref in enumerate((a1, b1, a2, b2, a3)):
            acc += dot(ref[at, :], near_ref[i + 1], NT)
        acc_ref[at, :] = acc


def second_kernel(acc_ref, a4, w_ref, out_ref):
    half = acc_ref.shape[0] // 2
    for part in range(2):
        at = pl.ds(part * half, half)
        out_ref[at, :] = acc_ref[at, :] + dot(a4[at, :], w_ref[0], NT)


def late_kernel(heads, acc_ref, a4, b3, w_ref, qw_ref, ga_ref, own_ref, theirs_ref):
    half = acc_ref.shape[0]
    for part in range(1):
        at = pl.ds(part * half, half)
        ga_ref[at, :] = (
            acc_ref[at, :] + dot(a4[at, :], w_ref[0], NT) + dot(b3[at, :], w_ref[1], NT)
        ).astype(jnp.bfloat16)
    for position in range(heads):
        h = lax.rem(core_index() * (heads // 2) + position, heads)
        both = dot(qw_ref[h], ga_ref[:, head_columns(position)], NN)
        to = own_ref if position < heads // 2 else theirs_ref
        to[pl.ds(position % (heads // 2) * DH, DH), :] = both[:DH] + both[DH:]


def gate_kernel(x_ref, *refs):
    refs[-1][...] = x_ref[...]


def core_index():
    return lax.rem(lax.axis_index("seq"), 2)


def x_index():
    return lax.rem(lax.div(lax.axis_index("seq"), 2), 4)


def y_index():
    return lax.div(lax.axis_index("seq"), 8)


def one_row(tile, i):
    return jnp.sum(jnp.where(lax.broadcasted_iota(jnp.int32, tile.shape, 0) == i, tile, 0.0), axis=0, keepdims=True)


def tail_of(totals):
    parts = [[p.astype(jnp.float32) for p in pieces(t, 3)] for t in totals]
    at = lax.broadcasted_iota(jnp.int32, (16, DH), 0)
    out = jnp.zeros((16, DH), jnp.float32)
    for j, three in enumerate(parts):
        for i, part in enumerate(three):
            out = jnp.where(at == 3 * j + i, part, out)
    return out.astype(jnp.bfloat16)


def total_in(tail, j):
    tail = tail.astype(jnp.float32)
    return one_row(tail, 3 * j) + one_row(tail, 3 * j + 1) + one_row(tail, 3 * j + 2)


def chip_key_kernel(heads, key_ref, key_other, tie_ref, sent_ref, chip_ref, tied_ref):
    tied_ref[...] = tie_ref[...]
    core = core_index()
    pair = heads // 2
    first = core == 0
    totals = []
    for j in range(pair):
        h = core * pair + j
        mine = one_row(key_ref[heads * DH :, :], h)
        others = one_row(key_other[heads * DH :, :], h)
        totals.append(mine + others)
        at = pl.ds(pl.multiple_of(h * DH, DH), DH)
        key = jnp.where(first, jnp.exp(others), 1.0) * key_ref[at, :] + jnp.where(first, 1.0, jnp.exp(mine)) * key_other[at, :]
        chip_ref[pl.ds(j * DH, DH), :] = key
        sent_ref[pl.ds(j * DH, DH), :] = key.astype(jnp.bfloat16)
    sent_ref[pl.ds(pair * DH, 16), :] = tail_of(totals)


def chip_grad_kernel(heads, key_ref, key_other, grad_ref, grad_other, sent_ref, chip_ref):
    core = core_index()
    pair = heads // 2
    first = core == 0
    for j in range(pair):
        h = core * pair + j
        mine = jnp.exp(one_row(key_ref[heads * DH :, :], h))
        others = jnp.exp(one_row(key_other[heads * DH :, :], h))
        at = pl.ds(j * DH, DH)
        grad = jnp.where(first, 1.0, others) * grad_ref[at, :] + jnp.where(first, mine, 1.0) * grad_other[at, :]
        chip_ref[pl.ds(j * DH, DH), :] = grad
        sent_ref[pl.ds(j * DH, DH), :] = grad.astype(jnp.bfloat16)


def flag(condition):
    return jnp.where(condition, 1.0, 0.0)


def places(x):
    return [jnp.bitwise_xor(x, d) for d in range(4)]


def between(totals, place, low, high):
    return sum(t * flag((low < p) & (p < high)) for t, p in zip(totals, place))


def row_key_kernel(pair, sent_ref, chip_ref, r1, r3, r2, in_ref, whole_ref, table_ref, tail_ref):
    x = x_index()
    n = pair * DH
    refs = (sent_ref, r1, r2, r3)
    place = places(x)
    tails = [ref[pl.ds(n, 16), :] for ref in refs]
    row_totals = []
    for j in range(pair):
        totals = [total_in(tail, j) for tail in tails]
        at = pl.ds(j * DH, DH)
        inside = 0.0
        whole = jnp.exp(between(totals, place, x, 4)) * chip_ref[at, :]
        for d in range(1, 4):
            state = refs[d][at, :].astype(jnp.float32)
            whole += jnp.exp(between(totals, place, place[d], 4)) * state
            inside += jnp.exp(between(totals, place, place[d], x)) * flag(place[d] < x) * state
        in_ref[at, :] = inside
        whole_ref[at, :] = whole
        lines = [jnp.exp(between(totals, place, -1, p)) for p in place]
        lines += [jnp.exp(between(totals, place, x, p)) * flag(p > x) for p in place[1:]]
        lines += [jnp.exp(between(totals, place, -1, x)), jnp.exp(between(totals, place, x, 4))]
        for i, line in enumerate(lines):
            table_ref[pl.ds(16 * j + i, 1), :] = line
        table_ref[pl.ds(16 * j + 9, 7), :] = jnp.zeros((7, DH), jnp.float32)
        row_totals.append(sum(totals))
    tail_ref[...] = tail_of(row_totals)


def row_grad_kernel(pair, chip_ref, r1, r3, r2, whole_key, table_ref, tail_ref, _, in_ref, s1, s2, s3):
    y = y_index()
    n = pair * DH
    refs = (r1, r2, r3)

    def line(j, i):
        return table_ref[pl.ds(16 * j + i, 1), :]

    for j in range(pair):
        at = pl.ds(j * DH, DH)
        inside = 0.0
        whole = line(j, 0) * chip_ref[at, :]
        for d in range(3):
            state = refs[d][at, :].astype(jnp.float32)
            whole += line(j, 1 + d) * state
            inside += line(j, 4 + d) * state
        in_ref[at, :] = inside
        for dy, ref in ((1, s1), (2, s2), (3, s3)):
            ref[at, :] = jnp.where(jnp.bitwise_xor(y, dy) > y, whole_key[at, :], whole).astype(jnp.bfloat16)
    for ref in (s1, s2, s3):
        ref[pl.ds(n, 16), :] = tail_ref[...]


def enter_kernel(pair, key_in, grad_in, table_ref, r2, r1, r3, _, enter_ref):
    y = y_index()
    n = pair * DH
    refs = (r1, r2, r3)
    place = places(y)[1:]
    tails = [ref[pl.ds(n, 16), :] for ref in refs]
    for j in range(pair):
        totals = [total_in(tail, j) for tail in tails]
        at = pl.ds(j * DH, DH)
        key, grad = key_in[at, :], grad_in[at, :]
        into, out = table_ref[pl.ds(16 * j + 7, 1), :], table_ref[pl.ds(16 * j + 8, 1), :]
        for d in range(3):
            p = place[d]
            gap = sum(t * flag(((p < q) & (q < y)) | ((y < q) & (q < p))) for t, q in zip(totals, place))
            weight = jnp.exp(gap)
            state = refs[d][at, :].astype(jnp.float32)
            key += into * weight * flag(p < y) * state
            grad += out * weight * flag(p > y) * state
        enter_ref[at, :] = key
        enter_ref[pl.ds((pair + j) * DH, DH), :] = grad


def closed(first, i, part, enter_ref, key_other, grad_other, ga_ref, k_ref, v_ref, start_w, end_w, dq, dk, dv, states):
    core = core_index()
    heads = key_other.shape[0] // DH
    pair = heads // 2
    cols = head_columns(first + i)
    if i not in states:
        h = lax.rem(core * pair + first + i, heads)
        key = enter_ref[pl.ds(i * DH, DH), :]
        grad = enter_ref[pl.ds((pair + i) * DH, DH), :]
        decay = jnp.exp(one_row(key_other[heads * DH :, :], h))
        si = jnp.where(core == 0, key, decay * key + key_other[cols, :])
        so = jnp.where(core == 0, decay * grad + grad_other[pl.ds(i * DH, DH), :], grad)
        hi, lo = pieces(so, 2)
        states[i] = jnp.concatenate(pieces(si, 2), axis=0), jnp.concatenate([hi, lo], axis=0), jnp.concatenate([hi, lo], axis=1)
    si, so, so_wide = states[i]
    mine = slice(i * DH, (i + 1) * DH)
    step = ga_ref.shape[0] // 4
    rows = pl.ds(part * step, step)

    def fold(x):
        return x[:, :DH] + x[:, DH:]

    return (
        dq[rows, mine] + start_w[rows, mine] * fold(dot(ga_ref[rows, cols], si, NT)),
        dk[rows, mine] + end_w[rows, mine] * fold(dot(v_ref[rows, cols], so, NT)),
        dv[rows, mine] + end_w[rows, mine] * fold(dot(k_ref[rows, cols], so_wide, NN)),
    )


def own_kernel(first, *refs):
    *inputs, out_ref = refs
    step = out_ref.shape[2] // 4
    states = {}
    for i in range(out_ref.shape[1]):
        for part in range(4):
            for j, value in enumerate(closed(first, i, part, *inputs, states)):
                out_ref[j, i, pl.ds(part * step, step)] = value


def rest_kernel(first, *refs):
    *inputs, own_ref, gq_ref, gk_ref, gv_ref, room, sems = refs
    outs = (gq_ref, gk_ref, gv_ref)
    pair, n = own_ref.shape[1:3]
    step = n // 4
    copies = []

    def send(src, j, position, at, sem):
        copy = pltpu.make_async_copy(src, outs[j].at[at, head_columns(position)], sem)
        copy.start()
        copies.append(copy)

    for i in range(pair):
        for j in range(3):
            send(own_ref.at[j, i], j, i, pl.ds(0, n), sems.at[j, i])
    states = {}
    for i in range(pair):
        for part in range(4):
            for j, value in enumerate(closed(first, i, part, *inputs, states)):
                room[j, i, pl.ds(part * step, step)] = value
            if part % 2:
                at = pl.ds((part - 1) * step, 2 * step)
                for j in range(3):
                    send(room.at[j, i, at], j, first + i, at, sems.at[j, pair + 2 * i + part // 2])
    for copy in copies:
        copy.wait()


def local(queries, keys, values, log_decay, out_weight, grad_out):
    rows, width = queries.shape
    heads = log_decay.shape[0]
    pair = heads // 2

    def along_z(array):
        pairs = []
        for i in range(32):
            for j in range(8):
                pairs.append((i * 8 + j, i * 8 + (j + (1 if i % 2 == 0 else -1)) % 8))
        return lax.ppermute(array, ("seq", "head"), pairs)

    def along_seq(array, dy=0, dx=0, flip=False):
        pairs = []
        for i in range(32):
            a, b, c = i // 8, (i // 2) % 4, i % 2
            pairs.append((i, (a ^ dy) * 8 + (b ^ dx) * 2 + (1 - c if flip else c)))
        return lax.ppermute(array, "seq", pairs)

    def other(array):
        return along_seq(array, flip=True)

    def in_hbm(array):
        return pltpu.with_memory_space_constraint(array, pltpu.HBM)

    b0 = other(grad_out)
    tie0 = jnp.zeros((8, DH), jnp.float32)
    key_own, _ = call(
        functools.partial(open_kernel, heads), (f32(heads * DH + 8, DH), f32(8, DH)),
        in_hbm(keys), in_hbm(values), in_hbm(log_decay), tie0,
        specs=[ANY] * 3 + [VMEM],
        scratch=[pltpu.VMEM((rows, width), jnp.bfloat16)] * 2 + [pltpu.VMEM((heads, rows), jnp.float32), pltpu.SemaphoreType.DMA((3,))],
    )
    a1 = along_z(grad_out)
    b1 = along_z(b0)

    key_other = other(key_own)
    sent, chip, b1 = call(
        functools.partial(chip_key_kernel, heads), (bf16(pair * DH + 16, DH), f32(pair * DH, DH), bf16(*grad_out.shape)),
        key_own, key_other, b1, specs=[VMEM] * 3,
    )
    from_x = [along_seq(sent, dx=d) for d in (2, 1, 3)]
    from_x = [from_x[1], from_x[0], from_x[2]]
    a2 = along_z(a1)
    b2 = along_z(b1)
    b2_here = other(b2)
    b1_here = other(call(gate_kernel, (bf16(*grad_out.shape),), b1, b2)[0])
    key_in, key_row, table, tail = call(
        functools.partial(row_key_kernel, pair),
        (f32(pair * DH, DH), f32(pair * DH, DH), f32(16 * pair, DH), bf16(16, DH)),
        sent, chip, from_x[0], from_x[2], from_x[1], specs=[VMEM] * 5,
    )
    a3 = along_z(a2)
    b3 = along_z(call(gate_kernel, (bf16(*grad_out.shape),), b2, from_x[0], from_x[2], from_x[1])[0])
    a4 = along_z(a3)

    qd = grad_out.shape[1]
    acc, w, qw, row, col = call(
        first_kernel,
        (f32(rows, width), bf16(2, width, qd), bf16(heads, 2 * DH, rows), f32(heads, rows), f32(rows, heads)),
        in_hbm(out_weight), in_hbm(grad_out), in_hbm(queries), in_hbm(log_decay), a1, b1_here, a2, b2_here, a3, tail,
        specs=[ANY] * 4 + [VMEM] * 6,
        scratch=[
            pltpu.VMEM((6, width, qd), jnp.bfloat16), pltpu.VMEM((rows, qd), jnp.bfloat16),
            pltpu.VMEM((rows, width), jnp.bfloat16), pltpu.VMEM((heads, rows), jnp.float32), pltpu.SemaphoreType.DMA((11,)),
        ],
    )
    b3_here = other(call(gate_kernel, (bf16(*grad_out.shape),), b3, acc)[0])
    ga, grad_own, grad_theirs = call(
        functools.partial(late_kernel, heads), (bf16(rows, width), f32(pair * DH, DH), f32(pair * DH, DH)), acc, a4, b3_here, w, qw
    )

    grad_other = other(grad_theirs)
    grad_rest = other(grad_own)
    sent, chip = call(
        functools.partial(chip_grad_kernel, heads), (bf16(pair * DH, DH), f32(pair * DH, DH)),
        key_own, key_other, grad_own, grad_other, specs=[VMEM] * 4,
    )
    from_x = [along_seq(sent, dx=d) for d in (2, 1, 3)]
    from_x = [from_x[1], from_x[0], from_x[2]]
    def local_part(first, after):
        *parts, tie = call(
            functools.partial(local_kernel, pair, first), (f32(rows, pair * DH),) * 5 + (f32(8, DH),),
            after, queries, keys, values, ga, row, col,
        )
        dq, dk, dv, start_w, end_w = parts
        return (start_w, end_w, dq, dk, dv), tie

    low, tie = local_part(0, row)
    high, tie_high = local_part(pair, grad_rest)
    grad_in, *sent = call(
        functools.partial(row_grad_kernel, pair),
        (f32(pair * DH, DH),) + (bf16(pair * DH + 16, DH),) * 3,
        chip, from_x[0], from_x[2], from_x[1], key_row, table, tail, tie, specs=[VMEM] * 8,
    )
    from_y = [along_seq(sent[d - 1], dy=d) for d in (2, 1, 3)]
    from_y = [from_y[1], from_y[0], from_y[2]]
    (enter,) = call(
        functools.partial(enter_kernel, pair), (f32(2 * pair * DH, DH),),
        key_in, grad_in, table, from_y[1], from_y[0], from_y[2], tie_high, specs=[VMEM] * 7,
    )
    enter_other = other(enter)

    (own,) = call(
        functools.partial(own_kernel, 0), (f32(3, pair, rows, DH),), enter, key_other, grad_other, ga, keys, values, *low
    )
    return pl.pallas_call(
        functools.partial(rest_kernel, pair),
        out_shape=(f32(rows, width),) * 3,
        in_specs=[VMEM] * 12,
        out_specs=(ANY,) * 3,
        scratch_shapes=[pltpu.VMEM((3, pair, rows, DH), jnp.float32), pltpu.SemaphoreType.DMA((3, 3 * pair))],
        compiler_params=pltpu.CompilerParams(vmem_limit_bytes=24 * 2**20),
    )(enter_other, key_other, grad_rest, ga, keys, values, *high, own)


def solution(mesh):
    return jax.shard_map(
        local,
        mesh=mesh,
        in_specs=(
            P("seq", "head"),
            P("seq", "head"),
            P("seq", "head"),
            P("head", "seq"),
            P("head", None),
            P("seq", "head"),
        ),
        out_specs=(P("seq", "head"), P("seq", "head"), P("seq", "head")),
        check_vma=False,
    )
```
